32 devices in a mesh: grp: 2 (over x), row: 8 (over z, y), col: 2 (over core).
Axes of the slice: x: 2, y: 2, z: 4, core: 2. Of those that a mesh axis runs over, the one named last changes fastest.
Arguments:
- pair: bfloat16 [512, 256, 128], P(('grp', 'row'), 'col'), parts along dimension 0, may hold values from -6 to 6
- length: int32 [2], P('grp'), parts along dimension 0, may hold values from 128 to 256
- norm_in_gain: float32 [128], replicated, may hold values from 0.5 to 1.5
- norm_in_bias: float32 [128], replicated, may hold values from -3 to 3
- proj_in: bfloat16 [128, 256], replicated, may hold values from -0.5 to 0.5
- gate_in: bfloat16 [128, 256], replicated, may hold values from -0.5 to 0.5
- gate_out: bfloat16 [128, 128], replicated, may hold values from -0.5 to 0.5
- norm_out_gain: float32 [128], replicated, may hold values from 0.5 to 1.5
- norm_out_bias: float32 [128], replicated, may hold values from -3 to 3
- proj_out: bfloat16 [128, 128], replicated, may hold values from -0.5 to 0.5
Outputs:
- update: bfloat16 [512, 256, 128], P(('grp', 'row'), 'col'), parts along dimension 0
The draws below stay inside these ranges and needn't reach their ends.
There are 2 independent parts, one for each index of `grp`. The reference program is written for one: setup_inputs(seed, part) draws one part's arguments, and reference() takes and returns one part's arrays. A program takes and returns all parts, laid end to end along the dimension named above; an argument that names none is the same for every part. Nothing has to cross between parts.
All inputs are finite; a program needn't handle non-finite values.
Results may differ from the reference program's by a relative error of at most 0.0059.
Values may be sent and summed in bfloat16 or wider, within the bound.
No kernel may reach another device: no remote copies, remote signals or barrier semaphores. Data moves between devices by JAX's collectives and lax.ppermute only.
A program may use at most 64 MiB of HBM per device.

```python
import jax
import jax.numpy as jnp
from jax import lax

PAIR_C = 128
TRI_H = 128
TOKENS = 256


def shard_levels(own_key, dims, shards, smallest, top_value):
    level, own = 1.0, jax.random.fold_in(own_key, 6)
    for axis_at, blocks in shards:
        draws = jnp.exp(jax.random.uniform(jax.random.fold_in(own, axis_at), (blocks,), jnp.float32, smallest / len(shards), top_value / len(shards)))
        level = level * jnp.repeat(draws, dims[axis_at] // blocks).reshape([-1 if axis == axis_at else 1 for axis in range(len(dims))])
    return level


def bell_draw(key, dims, deviation, reach, cuts=(), held_as=jnp.bfloat16):
    drawn = deviation * jax.random.normal(key, dims, jnp.float32)
    if cuts:
        drawn = drawn * shard_levels(key, dims, cuts, -0.22, 0.18)
    return jnp.clip(drawn, -reach, reach).astype(held_as)


def setup_inputs(seed: int = 0, part: int = 0) -> dict:
    keys = jax.random.split(jax.random.key(seed), 11)
    own_keys = jax.random.split(jax.random.fold_in(keys[10], part), 11)
    pair = bell_draw(own_keys[0], (TOKENS, TOKENS, PAIR_C), 1.0, 6.0, ((0, 8), (1, 2)))
    length = jax.random.randint(own_keys[1], (1,), TOKENS // 2, TOKENS + 1).astype(jnp.int32)
    norm_in_gain = jnp.clip(jax.random.uniform(keys[2], (PAIR_C,), jnp.float32, 0.5, 1.5), 0.5, 1.5)
    norm_in_bias = bell_draw(keys[3], (PAIR_C,), 0.5, 3.0, (), jnp.float32)
    proj_in = bell_draw(keys[4], (PAIR_C, 2 * TRI_H), PAIR_C ** -0.5, 0.5)
    gate_in = bell_draw(keys[5], (PAIR_C, 2 * TRI_H), PAIR_C ** -0.5, 0.5)
    gate_out = bell_draw(keys[6], (PAIR_C, PAIR_C), PAIR_C ** -0.5, 0.5)
    norm_out_gain = jnp.clip(jax.random.uniform(keys[7], (TRI_H,), jnp.float32, 0.5, 1.5), 0.5, 1.5)
    norm_out_bias = bell_draw(keys[8], (TRI_H,), 0.5, 3.0, (), jnp.float32)
    proj_out = bell_draw(keys[9], (TRI_H, PAIR_C), TRI_H ** -0.5, 0.5)
    return {"pair": pair, "length": length, "norm_in_gain": norm_in_gain, "norm_in_bias": norm_in_bias, "proj_in": proj_in, "gate_in": gate_in, "gate_out": gate_out, "norm_out_gain": norm_out_gain, "norm_out_bias": norm_out_bias, "proj_out": proj_out}


epsilon = 1e-05

def layer_norm(values, scale_vec, shift_vec):
    average = lax.optimization_barrier(jnp.mean(values, axis=-1, keepdims=True))
    centered = values - average
    spread = lax.optimization_barrier(jnp.mean(centered * centered, axis=-1, keepdims=True))
    return centered * jax.lax.rsqrt(spread + epsilon) * scale_vec + shift_vec

def reference(pair, length, norm_in_gain, norm_in_bias, proj_in, gate_in, gate_out, norm_out_gain, norm_out_bias, proj_out):
    normed = layer_norm(pair.astype(jnp.float32), norm_in_gain, norm_in_bias).astype(jnp.bfloat16)
    positions = jnp.arange(TOKENS, dtype=jnp.int32)
    valid = (positions < length[0]).astype(jnp.float32)
    pair_mask = valid[:, None] * valid[None, :]
    projected = jnp.dot(normed, proj_in, preferred_element_type=jnp.float32)
    gating = jnp.dot(normed, gate_in, preferred_element_type=jnp.float32)
    edges = (jax.nn.sigmoid(gating) * projected * pair_mask[:, :, None]).astype(jnp.bfloat16)
    left_edge = edges[:, :, :TRI_H].astype(jnp.float32)
    right_edge = edges[:, :, TRI_H:].astype(jnp.float32)
    contracted = jnp.einsum('kih,kjh->ijh', left_edge, right_edge).astype(jnp.bfloat16)
    contracted_norm = layer_norm(contracted.astype(jnp.float32), norm_out_gain, norm_out_bias).astype(jnp.bfloat16)
    out_gate = jax.nn.sigmoid(jnp.dot(normed, gate_out, preferred_element_type=jnp.float32))
    projected_out = jnp.dot(contracted_norm, proj_out, preferred_element_type=jnp.float32)
    return (out_gate * projected_out).astype(jnp.bfloat16)
```

```python
import functools

import jax
import jax.numpy as jnp
from jax import lax
from jax.experimental import pallas as pl
from jax.experimental.pallas import tpu as pltpu
from jax.sharding import PartitionSpec as P

epsilon = 1e-05
chunk_sizes = (12, 20)
swap_pieces = (1, 2)
vmem_all = 60 * 1024 * 1024
vmem_part = 28 * 1024 * 1024


def from_partner(value, axis, apart):
    mask = 2**apart
    pairs = [(source, source ^ mask) for source in range(lax.axis_size(axis))]
    return lax.ppermute(value, axis, pairs)


def normalize_in(pair, gain, bias):
    widened = pair.astype(jnp.float32)
    average = jnp.mean(widened, axis=-1, keepdims=True)
    centered = widened - average
    spread = jnp.mean(centered * centered, axis=-1, keepdims=True)
    return (centered * lax.rsqrt(spread + epsilon) * gain + bias).astype(jnp.bfloat16)


def token_mask(tile_rows, tile_cols, length):
    row_start = lax.axis_index("row") * tile_rows
    col_start = lax.axis_index("col") * tile_cols
    valid_rows = row_start + jnp.arange(tile_rows, dtype=jnp.int32) < length[0]
    valid_cols = col_start + jnp.arange(tile_cols, dtype=jnp.int32) < length[0]
    return (valid_rows[:, None] & valid_cols[None, :]).astype(jnp.float32)


def make_edges(normed, proj, gate, mask):
    projected = jnp.einsum("ijc,ch->hij", normed, proj, preferred_element_type=jnp.float32)
    gating = jnp.einsum("ijc,ch->hij", normed, gate, preferred_element_type=jnp.float32)
    return (jax.nn.sigmoid(gating) * projected * mask[None]).astype(jnp.bfloat16)


def finish(contracted, normed, gate_out, gain, bias, proj_out):
    widened = contracted.astype(jnp.float32)
    average = jnp.mean(widened, axis=0, keepdims=True)
    centered = widened - average
    spread = jnp.mean(centered * centered, axis=0, keepdims=True)
    scaled = centered * lax.rsqrt(spread + epsilon) * gain[:, None, None]
    contracted_norm = (scaled + bias[:, None, None]).astype(jnp.bfloat16)
    out_gate = jax.nn.sigmoid(
        jnp.einsum("ijc,cd->ijd", normed, gate_out, preferred_element_type=jnp.float32)
    )
    projected_out = jnp.einsum(
        "hij,hc->ijc", contracted_norm, proj_out, preferred_element_type=jnp.float32
    )
    return (out_gate * projected_out).astype(jnp.bfloat16)


def contract(left, right):
    return jnp.einsum("hki,hkj->hij", left, right, preferred_element_type=jnp.float32)


def shards_by_exchange(
    pair,
    length,
    norm_in_gain,
    norm_in_bias,
    proj_in,
    gate_in,
    gate_out,
    norm_out_gain,
    norm_out_bias,
    proj_out,
):
    hidden = proj_out.shape[0]
    normed = normalize_in(pair, norm_in_gain, norm_in_bias)
    mask = token_mask(pair.shape[0], pair.shape[1], length)
    edges = make_edges(normed, proj_in, gate_in, mask)
    left_rows = lax.all_to_all(edges[:hidden], "row", split_axis=0, concat_axis=1, tiled=True)
    right_rows = lax.all_to_all(edges[hidden:], "row", split_axis=0, concat_axis=1, tiled=True)
    other_half = from_partner(left_rows, "col", 0)
    first_col = lax.axis_index("col") == 0
    left_full = jnp.where(
        first_col,
        jnp.concatenate([left_rows, other_half], axis=2),
        jnp.concatenate([other_half, left_rows], axis=2),
    )
    contracted = contract(left_full, right_rows).astype(jnp.bfloat16)
    returned = lax.all_to_all(contracted, "row", split_axis=1, concat_axis=0, tiled=True)
    return finish(returned, normed, gate_out, norm_out_gain, norm_out_bias, proj_out)


in_smem = pl.BlockSpec(memory_space=pltpu.SMEM)
in_any = pl.BlockSpec(memory_space=pl.ANY)
matmul_tn = (((0,), (0,)), ((), ()))
matmul_nt = (((1,), (1,)), ((), ()))


def call(kernel, outputs, scratch, specs, name, limit=vmem_part):
    return pl.pallas_call(
        kernel,
        out_shape=outputs,
        in_specs=specs,
        out_specs=[in_any] * len(outputs),
        scratch_shapes=scratch,
        compiler_params=pltpu.CompilerParams(vmem_limit_bytes=limit),
        cost_estimate=pl.CostEstimate(flops=0, bytes_accessed=1024, transcendentals=0),
        name=name,
    )


def array(shape, dtype=jnp.bfloat16):
    return jax.ShapeDtypeStruct(shape, dtype)


def load(source, target, sem):
    copy = pltpu.make_async_copy(source, target, sem)
    copy.start()
    return copy


def transposed_weights(proj, gate, held):
    width = proj.shape[1]
    held[pl.ds(0, width), :] = proj[...].astype(jnp.float32).T.astype(jnp.bfloat16)
    held[pl.ds(width, width), :] = gate[...].astype(jnp.float32).T.astype(jnp.bfloat16)


def chunk_weights(held, start, stop):
    width = held.shape[0] // 2
    hidden = width // 2
    offsets = (0, hidden, width, width + hidden)
    return jnp.concatenate([held[offset + start : offset + stop, :] for offset in offsets], axis=0)


def block_edges(length, normed, weights, at, row_start, col_start, out):
    rows, tile_cols, channels = normed.shape
    slots, both, _, _ = out.shape
    size = both // 2
    pairs = lax.dot_general(
        weights,
        normed.reshape(rows * tile_cols, channels),
        matmul_nt,
        preferred_element_type=jnp.float32,
    )
    count = pairs.shape[0] // 2
    values = jax.nn.sigmoid(pairs[count:]) * pairs[:count]
    cols = col_start + lax.broadcasted_iota(jnp.int32, (count, tile_cols), 1)
    masked = []
    for row in range(rows):
        limit = jnp.where(row_start + at + row < length, length, 0)
        piece = values[:, row * tile_cols : (row + 1) * tile_cols]
        masked.append(jnp.where(cols < limit, piece, 0.0))
    swapped = jnp.swapaxes(jnp.stack(masked, axis=0), 0, 1).astype(jnp.bfloat16)
    for slot in range(slots):
        for side in range(2):
            first = (side * slots + slot) * size
            out[slot, side * size : (side + 1) * size, at : at + rows, :] = swapped[
                first : first + size
            ]


def first_kernel(bounds, length, pair, gain, bias, proj, gate, normed, *rest):
    start, stop, rows = bounds
    outs = rest[:4]
    pair_held, gain_held, bias_held, proj_held, gate_held, weights_held = rest[4:10]
    normed_held, out_held, sems = rest[10:]
    tile_rows, tile_cols, channels = pair.shape
    blocks = tile_rows // rows
    small = [
        load(source, target, sems.at[at])
        for at, (source, target) in enumerate(
            ((proj, proj_held), (gate, gate_held), (gain, gain_held), (bias, bias_held))
        )
    ]
    pieces = [
        load(pair.at[pl.ds(b * rows, rows)], pair_held.at[pl.ds(b * rows, rows)], sems.at[4 + b])
        for b in range(blocks)
    ]
    row = lax.axis_index("row")
    row_start = row * tile_rows
    col_start = lax.axis_index("col") * tile_cols
    for copy in small:
        copy.wait()
    transposed_weights(proj_held, gate_held, weights_held)
    weights = chunk_weights(weights_held, start, stop)
    for b in range(blocks):
        at = b * rows
        pieces[b].wait()
        widened = pair_held[at : at + rows].astype(jnp.float32).reshape(rows * tile_cols, channels)
        average = jnp.mean(widened, axis=-1, keepdims=True)
        centered = widened - average
        spread = jnp.mean(centered * centered, axis=-1, keepdims=True)
        scaled = centered * lax.rsqrt(spread + epsilon) * gain_held[...] + bias_held[...]
        rounded = scaled.astype(jnp.bfloat16).reshape(rows, tile_cols, channels)
        normed_held[at : at + rows] = rounded
        block_edges(length[0], rounded, weights, at, row_start, col_start, out_held)
    base = 4 + blocks
    stores = [load(normed_held, normed, sems.at[base])]
    for slot, out in enumerate(outs):
        stores.append(load(out_held.at[(row % 4) ^ slot], out, sems.at[base + 1 + slot]))
    for copy in stores:
        copy.wait()


def later_kernel(bounds, length, normed, proj, gate, *rest):
    start, stop, rows = bounds
    outs = rest[:4]
    normed_held, proj_held, gate_held, weights_held, out_held, sems = rest[4:]
    tile_rows = normed.shape[0]
    blocks = tile_rows // rows
    loads = [
        load(source, target, sems.at[at])
        for at, (source, target) in enumerate(
            ((proj, proj_held), (gate, gate_held), (normed, normed_held))
        )
    ]
    row = lax.axis_index("row")
    row_start = row * tile_rows
    col_start = lax.axis_index("col") * normed.shape[1]
    loads[0].wait()
    loads[1].wait()
    transposed_weights(proj_held, gate_held, weights_held)
    weights = chunk_weights(weights_held, start, stop)
    loads[2].wait()
    for b in range(blocks):
        at = b * rows
        tokens = normed_held[at : at + rows]
        block_edges(length[0], tokens, weights, at, row_start, col_start, out_held)
    stores = [
        load(out_held.at[(row % 4) ^ slot], out, sems.at[3 + slot]) for slot, out in enumerate(outs)
    ]
    for copy in stores:
        copy.wait()


def gate_kernel(rows, after, normed, weights, out, normed_held, weights_held, out_held, sems):
    tile_rows, tile_cols, channels = normed.shape
    load(weights, weights_held, sems.at[0]).wait()
    load(normed, normed_held, sems.at[1]).wait()
    stores = []
    for b in range(tile_rows // rows):
        at = b * rows
        gating = jnp.dot(
            normed_held[at : at + rows].reshape(rows * tile_cols, channels),
            weights_held[...],
            preferred_element_type=jnp.float32,
        )
        out_held[at : at + rows] = jax.nn.sigmoid(gating).reshape(rows, tile_cols, channels)
        part = pl.ds(at, rows)
        stores.append(load(out_held.at[part], out.at[part], sems.at[2 + b]))
    for copy in stores:
        copy.wait()


def pack_kernel(after, a, b, c, d, *rest):
    outs, sems = rest[:-1], rest[-1]
    size, count, _ = outs[0].shape
    part = count // 4
    copies = []
    for piece, out in enumerate(outs):
        for at, ref in enumerate((a, b, c, d)):
            rows = out.at[:, pl.ds(at * part, part), :]
            copies.append(load(ref.at[pl.ds(piece * size, size)], rows, sems.at[piece, at]))
    for copy in copies:
        copy.wait()


def products(lefts, parts, left_held, right_held, sems, outs):
    _, size, depth, _ = left_held.shape
    part = depth // 4
    row, col = lax.axis_index("row"), lax.axis_index("col")
    loads, start = [], 0
    for at in range(len(lefts) // 2):
        count = lefts[2 * at].shape[0]
        which = pl.ds(start, count)
        loads.append(load(lefts[2 * at], left_held.at[col, which], sems.at[len(loads)]))
        loads.append(load(lefts[2 * at + 1], left_held.at[1 - col, which], sems.at[len(loads)]))
        start += count
    for at, ref in enumerate(parts):
        loads.append(
            load(
                ref.at[pl.ds(size, size)],
                right_held.at[:, pl.ds(at * part, part), :],
                sems.at[len(loads)],
            )
        )
    low = (row < 4).astype(jnp.int32)
    for copy in loads:
        copy.wait()
    for side, held in ((low, outs[0]), (1 - low, outs[1])):
        for u in range(size):
            product = lax.dot_general(
                left_held[side, u], right_held[u], matmul_tn, preferred_element_type=jnp.float32
            )
            held[u] = product.astype(held.dtype)
        yield held


def contract_kernel(count, *refs):
    lefts, parts = refs[:count], refs[count : count + 4]
    away, keep, left_held, right_held, away_held, keep_held, sems = refs[count + 4 :]
    stores = []
    helds = (away_held, keep_held)
    for at, held in enumerate(products(lefts, parts, left_held, right_held, sems, helds)):
        stores.append(load(held, (away, keep)[at], sems.at[count + 4 + at]))
    for copy in stores:
        copy.wait()


def last_contract_kernel(count, *refs):
    lefts, parts = refs[:count], refs[count : count + 4]
    outs = refs[count + 4 : count + 8], refs[count + 8 : count + 12]
    left_held, right_held, away_held, keep_held, sems = refs[count + 12 :]
    part = left_held.shape[2] // 4
    row = lax.axis_index("row")
    stores = []
    helds = (away_held, keep_held)
    for half, held in enumerate(products(lefts, parts, left_held, right_held, sems, helds)):
        for slot, out in enumerate(outs[half]):
            rows = pl.ds(pl.multiple_of(((row % 4) ^ slot) * part, part), part)
            place = count + 4 + 4 * half + slot
            stores.append(load(held.at[:, rows, :], out, sems.at[place]))
    for copy in stores:
        copy.wait()


def add_kernel(keep, arrived, *refs):
    lasts, outs = refs[:4], refs[4:8]
    keep_held, arrived_held, sems = refs[8:]
    size, part = keep.shape[0], outs[0].shape[1]
    row = lax.axis_index("row")
    loads = [load(keep, keep_held, sems.at[0]), load(arrived, arrived_held, sems.at[1])]
    stores = [
        load(last, out.at[pl.ds(size, last.shape[0])], sems.at[2 + at])
        for at, (last, out) in enumerate(zip(lasts, outs, strict=True))
    ]
    for copy in loads:
        copy.wait()
    for u in range(size):
        total = keep_held[u] + arrived_held[u].astype(jnp.float32)
        arrived_held[u] = total.astype(jnp.bfloat16)
    for slot, out in enumerate(outs):
        rows = pl.ds(pl.multiple_of(((row % 4) ^ slot) * part, part), part)
        stores.append(
            load(arrived_held.at[:, rows, :], out.at[pl.ds(0, size)], sems.at[6 + slot])
        )
    for copy in stores:
        copy.wait()


def finish_kernel(rows, ranges, *refs):
    aways, totals = refs[:4], refs[4:8]
    opened, gain, bias, proj, out = refs[8:13]
    parts_held, last_held, opened_held, gain_held, bias_held, proj_held, out_held, sems = refs[13:]
    hidden, tile_rows, tile_cols = parts_held.shape
    last_start = ranges[-1][0]
    row = lax.axis_index("row")
    moves = [(gain, gain_held), (bias, bias_held), (proj, proj_held)]
    for slot in range(4):
        from_slot = (row % 4) ^ slot
        offset = 0
        for start, stop in ranges:
            size = (stop - start) // 4
            target = parts_held.at[pl.ds(start + from_slot * size, size)]
            moves.append((totals[slot].at[pl.ds(offset, size)], target))
            offset += size
        moves.append((aways[slot], last_held.at[pl.ds(from_slot * size, size)]))
    moves.append((opened, opened_held))
    loads = [load(source, target, sems.at[at]) for at, (source, target) in enumerate(moves)]
    for copy in loads[:-1]:
        copy.wait()
    gain_rows = jnp.broadcast_to(gain_held[...], (hidden, hidden)).T
    bias_rows = jnp.broadcast_to(bias_held[...], (hidden, hidden)).T
    zero = jnp.zeros((tile_rows, tile_cols), jnp.float32)

    def early(h):
        return parts_held[h].astype(jnp.float32)

    def late(h):
        return early(h) + last_held[h - last_start].astype(jnp.float32)

    def over_channels(step):
        done = lax.fori_loop(0, last_start, lambda h, s: s + step(early(h)), zero, unroll=8)
        done = lax.fori_loop(last_start, hidden, lambda h, s: s + step(late(h)), done, unroll=8)
        return done * (1.0 / hidden)

    average = over_channels(lambda value: value)
    spread = over_channels(lambda value: (value - average) * (value - average))
    scale = lax.rsqrt(spread + epsilon)
    stores = []
    loads[-1].wait()
    for b in range(tile_rows // rows):
        at = b * rows
        own = slice(at, at + rows)
        first = parts_held[:last_start, own, :].astype(jnp.float32)
        second = parts_held[last_start:, own, :].astype(jnp.float32)
        second = second + last_held[:, own, :].astype(jnp.float32)
        centered = jnp.concatenate([first, second], axis=0) - average[None, own]
        swapped = jnp.swapaxes(centered * scale[None, own], 0, 1)
        scaled = (swapped * gain_rows[None] + bias_rows[None]).astype(jnp.bfloat16)
        for step in range(rows):
            projected = lax.dot_general(
                scaled[step], proj_held[...], matmul_tn, preferred_element_type=jnp.float32
            )
            out_held[at + step] = (opened_held[at + step] * projected).astype(jnp.bfloat16)
        part = pl.ds(at, rows)
        stores.append(load(out_held.at[part], out.at[part], sems.at[len(moves) + b]))
    for copy in stores:
        copy.wait()


def shards_by_halves(
    pair,
    length,
    norm_in_gain,
    norm_in_bias,
    proj_in,
    gate_in,
    gate_out,
    norm_out_gain,
    norm_out_bias,
    proj_out,
):
    tile_rows, tile_cols, channels = pair.shape
    hidden = proj_out.shape[0]
    rows = lax.axis_size("row")
    block = min(16, tile_rows)
    blocks = tile_rows // block
    stops = [4 * sum(chunk_sizes[: at + 1]) for at in range(len(chunk_sizes))]
    ranges = list(zip([0, *stops[:-1]], stops, strict=True))
    wide = proj_in.shape[1]
    vmem, semaphores = pltpu.VMEM, pltpu.SemaphoreType.DMA
    small = jnp.bfloat16
    weights_scratch = [vmem(proj_in.shape, small), vmem(gate_in.shape, small)]
    turned = vmem((2 * wide, channels), small)
    depth = 4 * tile_rows

    def exchanged(value, mask):
        return lax.ppermute(value, "row", [(source, source ^ mask) for source in range(rows)])

    def edge_arrays(size):
        return [array((2 * size, tile_rows, tile_cols))] * 4

    def edge_scratch(size):
        return vmem((4, 2 * size, tile_rows, tile_cols), small)

    def edges_of(at, normed):
        return call(
            functools.partial(later_kernel, (*ranges[at], block)),
            edge_arrays(chunk_sizes[at]),
            [
                vmem(pair.shape, small),
                *weights_scratch,
                turned,
                edge_scratch(chunk_sizes[at]),
                semaphores((7,)),
            ],
            [in_smem] + [in_any] * 3,
            "later_edges",
        )(length, normed, proj_in, gate_in)

    def received(pieces):
        return [pieces[0], *[exchanged(pieces[mask], mask) for mask in (3, 2, 1)][::-1]]

    def swapped_left(at, after, pieces):
        size = chunk_sizes[at] // swap_pieces[at]
        lefts = call(
            pack_kernel,
            [array((size, depth, tile_cols))] * swap_pieces[at],
            [semaphores((swap_pieces[at], 4))],
            [in_any] * 5,
            "pack_left",
        )(after, *pieces)
        return [side for left in lefts for side in (left, from_partner(left, "col", 0))]

    def product_scratch(size, kept, count):
        shape = (size, depth, tile_cols)
        return [
            vmem((2, *shape), small),
            vmem(shape, small),
            vmem(shape, small),
            vmem(shape, kept),
            semaphores((count,)),
        ]

    def contracted(at, after, pieces):
        size = chunk_sizes[at]
        shape = (size, depth, tile_cols)
        lefts = swapped_left(at, after, pieces)
        return call(
            functools.partial(contract_kernel, len(lefts)),
            [array(shape), array(shape, jnp.float32)],
            product_scratch(size, jnp.float32, len(lefts) + 6),
            [in_any] * (len(lefts) + 4),
            "contract",
        )(*lefts, *pieces)

    def last_contracted(at, after, pieces):
        size = chunk_sizes[at]
        lefts = swapped_left(at, after, pieces)
        return call(
            functools.partial(last_contract_kernel, len(lefts)),
            [array((size, tile_rows, tile_cols))] * 8,
            product_scratch(size, small, len(lefts) + 12),
            [in_any] * (len(lefts) + 4),
            "contract",
        )(*lefts, *pieces)

    normed, *first = call(
        functools.partial(first_kernel, (*ranges[0], block)),
        [array(pair.shape), *edge_arrays(chunk_sizes[0])],
        [
            vmem(pair.shape, small),
            vmem((1, channels), jnp.float32),
            vmem((1, channels), jnp.float32),
            *weights_scratch,
            turned,
            vmem(pair.shape, small),
            edge_scratch(chunk_sizes[0]),
            semaphores((9 + blocks,)),
        ],
        [in_smem] + [in_any] * 5,
        "norm_and_first_edges",
        vmem_all,
    )(length, pair, norm_in_gain[None], norm_in_bias[None], proj_in, gate_in)
    first = received(first)
    second = edges_of(1, normed)
    away, keep = contracted(0, second[0], first)
    second = received(second)
    arrived = exchanged(away, 4)
    (opened,) = call(
        functools.partial(gate_kernel, block),
        [array(pair.shape, jnp.float32)],
        [
            vmem(pair.shape, small),
            vmem(gate_out.shape, small),
            vmem(pair.shape, jnp.float32),
            semaphores((2 + blocks,)),
        ],
        [in_any] * 3,
        "output_gate",
    )(away, normed, gate_out)
    last = last_contracted(1, opened, second)
    aways = [exchanged(last[mask], 4 ^ mask) for mask in range(4)]
    size = chunk_sizes[0]
    totals = call(
        add_kernel,
        [array((sum(chunk_sizes), tile_rows, tile_cols))] * 4,
        [
            vmem((size, depth, tile_cols), jnp.float32),
            vmem((size, depth, tile_cols), small),
            semaphores((10,)),
        ],
        [in_any] * 6,
        "add_halves",
    )(keep, arrived, *last[4:])
    totals = [totals[0], *[exchanged(totals[mask], mask) for mask in (1, 2, 3)]]
    (update,) = call(
        functools.partial(finish_kernel, 8, ranges),
        [array(pair.shape)],
        [
            vmem((hidden, tile_rows, tile_cols), small),
            vmem((4 * chunk_sizes[-1], tile_rows, tile_cols), small),
            vmem(pair.shape, jnp.float32),
            vmem((1, hidden), jnp.float32),
            vmem((1, hidden), jnp.float32),
            vmem(proj_out.shape, small),
            vmem(pair.shape, small),
            semaphores((4 + 4 * (len(ranges) + 1) + tile_rows // 8,)),
        ],
        [in_any] * 12,
        "norm_and_project_out",
    )(*aways, *totals, opened, norm_out_gain[None], norm_out_bias[None], proj_out)
    return update


def solution(mesh):
    placed = (P(("grp", "row"), "col", None), P("grp"), P(), P(), P(), P(), P(), P(), P(), P())
    return jax.shard_map(
        shards_by_halves if mesh.shape["row"] == 8 else shards_by_exchange,
        mesh=mesh,
        in_specs=placed,
        out_specs=P(("grp", "row"), "col", None),
        check_vma=False,
    )
```

```python
import functools

import jax
import jax.numpy as jnp
from jax import lax
from jax.experimental import pallas as pl
from jax.experimental.pallas import tpu as pltpu
from jax.sharding import PartitionSpec as P

epsilon = 1e-05
chunk_sizes = (12, 20)
swap_pieces = (2, 2)
vmem_all = 60 * 1024 * 1024
vmem_part = 28 * 1024 * 1024


def from_partner(value, axis, apart):
    mask = 2**apart
    pairs = [(source, source ^ mask) for source in range(lax.axis_size(axis))]
    return lax.ppermute(value, axis, pairs)


def normalize_in(pair, gain, bias):
    widened = pair.astype(jnp.float32)
    average = jnp.mean(widened, axis=-1, keepdims=True)
    centered = widened - average
    spread = jnp.mean(centered * centered, axis=-1, keepdims=True)
    return (centered * lax.rsqrt(spread + epsilon) * gain + bias).astype(jnp.bfloat16)


def token_mask(tile_rows, tile_cols, length):
    row_start = lax.axis_index("row") * tile_rows
    col_start = lax.axis_index("col") * tile_cols
    valid_rows = row_start + jnp.arange(tile_rows, dtype=jnp.int32) < length[0]
    valid_cols = col_start + jnp.arange(tile_cols, dtype=jnp.int32) < length[0]
    return (valid_rows[:, None] & valid_cols[None, :]).astype(jnp.float32)


def make_edges(normed, proj, gate, mask):
    projected = jnp.einsum("ijc,ch->hij", normed, proj, preferred_element_type=jnp.float32)
    gating = jnp.einsum("ijc,ch->hij", normed, gate, preferred_element_type=jnp.float32)
    return (jax.nn.sigmoid(gating) * projected * mask[None]).astype(jnp.bfloat16)


def finish(contracted, normed, gate_out, gain, bias, proj_out):
    widened = contracted.astype(jnp.float32)
    average = jnp.mean(widened, axis=0, keepdims=True)
    centered = widened - average
    spread = jnp.mean(centered * centered, axis=0, keepdims=True)
    scaled = centered * lax.rsqrt(spread + epsilon) * gain[:, None, None]
    contracted_norm = (scaled + bias[:, None, None]).astype(jnp.bfloat16)
    out_gate = jax.nn.sigmoid(
        jnp.einsum("ijc,cd->ijd", normed, gate_out, preferred_element_type=jnp.float32)
    )
    projected_out = jnp.einsum(
        "hij,hc->ijc", contracted_norm, proj_out, preferred_element_type=jnp.float32
    )
    return (out_gate * projected_out).astype(jnp.bfloat16)


def contract(left, right):
    return jnp.einsum("hki,hkj->hij", left, right, preferred_element_type=jnp.float32)


def shards_by_exchange(
    pair,
    length,
    norm_in_gain,
    norm_in_bias,
    proj_in,
    gate_in,
    gate_out,
    norm_out_gain,
    norm_out_bias,
    proj_out,
):
    hidden = proj_out.shape[0]
    normed = normalize_in(pair, norm_in_gain, norm_in_bias)
    mask = token_mask(pair.shape[0], pair.shape[1], length)
    edges = make_edges(normed, proj_in, gate_in, mask)
    left_rows = lax.all_to_all(edges[:hidden], "row", split_axis=0, concat_axis=1, tiled=True)
    right_rows = lax.all_to_all(edges[hidden:], "row", split_axis=0, concat_axis=1, tiled=True)
    other_half = from_partner(left_rows, "col", 0)
    first_col = lax.axis_index("col") == 0
    left_full = jnp.where(
        first_col,
        jnp.concatenate([left_rows, other_half], axis=2),
        jnp.concatenate([other_half, left_rows], axis=2),
    )
    contracted = contract(left_full, right_rows).astype(jnp.bfloat16)
    returned = lax.all_to_all(contracted, "row", split_axis=1, concat_axis=0, tiled=True)
    return finish(returned, normed, gate_out, norm_out_gain, norm_out_bias, proj_out)


in_smem = pl.BlockSpec(memory_space=pltpu.SMEM)
in_any = pl.BlockSpec(memory_space=pl.ANY)
matmul_tn = (((0,), (0,)), ((), ()))
matmul_nt = (((1,), (1,)), ((), ()))


def call(kernel, outputs, scratch, specs, name, limit=vmem_part):
    return pl.pallas_call(
        kernel,
        out_shape=outputs,
        in_specs=specs,
        out_specs=[in_any] * len(outputs),
        scratch_shapes=scratch,
        compiler_params=pltpu.CompilerParams(vmem_limit_bytes=limit),
        cost_estimate=pl.CostEstimate(flops=0, bytes_accessed=1024, transcendentals=0),
        name=name,
    )


def array(shape, dtype=jnp.bfloat16):
    return jax.ShapeDtypeStruct(shape, dtype)


def load(source, target, sem):
    copy = pltpu.make_async_copy(source, target, sem)
    copy.start()
    return copy


def transposed_weights(proj, gate, held):
    width = proj.shape[1]
    held[pl.ds(0, width), :] = proj[...].astype(jnp.float32).T.astype(jnp.bfloat16)
    held[pl.ds(width, width), :] = gate[...].astype(jnp.float32).T.astype(jnp.bfloat16)


def chunk_weights(held, start, stop):
    width = held.shape[0] // 2
    hidden = width // 2
    offsets = (0, hidden, width, width + hidden)
    return jnp.concatenate([held[offset + start : offset + stop, :] for offset in offsets], axis=0)


def block_edges(length, normed, weights, at, row_start, col_start, out):
    rows, tile_cols, channels = normed.shape
    slots, both, _, _ = out.shape
    size = both // 2
    pairs = lax.dot_general(
        weights,
        normed.reshape(rows * tile_cols, channels),
        matmul_nt,
        preferred_element_type=jnp.float32,
    )
    count = pairs.shape[0] // 2
    values = jax.nn.sigmoid(pairs[count:]) * pairs[:count]
    cols = col_start + lax.broadcasted_iota(jnp.int32, (count, tile_cols), 1)
    masked = []
    for row in range(rows):
        limit = jnp.where(row_start + at + row < length, length, 0)
        piece = values[:, row * tile_cols : (row + 1) * tile_cols]
        masked.append(jnp.where(cols < limit, piece, 0.0))
    swapped = jnp.swapaxes(jnp.stack(masked, axis=0), 0, 1).astype(jnp.bfloat16)
    for slot in range(slots):
        for side in range(2):
            first = (side * slots + slot) * size
            out[slot, side * size : (side + 1) * size, at : at + rows, :] = swapped[
                first : first + size
            ]


def first_kernel(bounds, length, pair, gain, bias, proj, gate, normed, *rest):
    start, stop, rows = bounds
    outs = rest[:4]
    pair_held, gain_held, bias_held, proj_held, gate_held, weights_held = rest[4:10]
    normed_held, out_held, sems = rest[10:]
    tile_rows, tile_cols, channels = pair.shape
    blocks = tile_rows // rows
    small = [
        load(source, target, sems.at[at])
        for at, (source, target) in enumerate(
            ((proj, proj_held), (gate, gate_held), (gain, gain_held), (bias, bias_held))
        )
    ]
    pieces = [
        load(pair.at[pl.ds(b * rows, rows)], pair_held.at[pl.ds(b * rows, rows)], sems.at[4 + b])
        for b in range(blocks)
    ]
    row = lax.axis_index("row")
    row_start = row * tile_rows
    col_start = lax.axis_index("col") * tile_cols
    for copy in small:
        copy.wait()
    transposed_weights(proj_held, gate_held, weights_held)
    weights = chunk_weights(weights_held, start, stop)
    for b in range(blocks):
        at = b * rows
        pieces[b].wait()
        widened = pair_held[at : at + rows].astype(jnp.float32).reshape(rows * tile_cols, channels)
        average = jnp.mean(widened, axis=-1, keepdims=True)
        centered = widened - average
        spread = jnp.mean(centered * centered, axis=-1, keepdims=True)
        scaled = centered * lax.rsqrt(spread + epsilon) * gain_held[...] + bias_held[...]
        rounded = scaled.astype(jnp.bfloat16).reshape(rows, tile_cols, channels)
        normed_held[at : at + rows] = rounded
        block_edges(length[0], rounded, weights, at, row_start, col_start, out_held)
    base = 4 + blocks
    stores = [load(normed_held, normed, sems.at[base])]
    for slot, out in enumerate(outs):
        stores.append(load(out_held.at[(row % 4) ^ slot], out, sems.at[base + 1 + slot]))
    for copy in stores:
        copy.wait()


def later_kernel(bounds, length, normed, proj, gate, *rest):
    start, stop, rows = bounds
    outs = rest[:4]
    normed_held, proj_held, gate_held, weights_held, out_held, sems = rest[4:]
    tile_rows = normed.shape[0]
    blocks = tile_rows // rows
    loads = [
        load(source, target, sems.at[at])
        for at, (source, target) in enumerate(
            ((proj, proj_held), (gate, gate_held), (normed, normed_held))
        )
    ]
    row = lax.axis_index("row")
    row_start = row * tile_rows
    col_start = lax.axis_index("col") * normed.shape[1]
    loads[0].wait()
    loads[1].wait()
    transposed_weights(proj_held, gate_held, weights_held)
    weights = chunk_weights(weights_held, start, stop)
    loads[2].wait()
    for b in range(blocks):
        at = b * rows
        tokens = normed_held[at : at + rows]
        block_edges(length[0], tokens, weights, at, row_start, col_start, out_held)
    stores = [
        load(out_held.at[(row % 4) ^ slot], out, sems.at[3 + slot]) for slot, out in enumerate(outs)
    ]
    for copy in stores:
        copy.wait()


def gate_kernel(rows, after, normed, weights, out, normed_held, weights_held, out_held, sems):
    tile_rows, tile_cols, channels = normed.shape
    load(weights, weights_held, sems.at[0]).wait()
    load(normed, normed_held, sems.at[1]).wait()
    stores = []
    for b in range(tile_rows // rows):
        at = b * rows
        gating = jnp.dot(
            normed_held[at : at + rows].reshape(rows * tile_cols, channels),
            weights_held[...],
            preferred_element_type=jnp.float32,
        )
        out_held[at : at + rows] = jax.nn.sigmoid(gating).reshape(rows, tile_cols, channels)
        part = pl.ds(at, rows)
        stores.append(load(out_held.at[part], out.at[part], sems.at[2 + b]))
    for copy in stores:
        copy.wait()


def pack_kernel(after, a, b, c, d, *rest):
    outs, sems = rest[:-1], rest[-1]
    size, count, _ = outs[0].shape
    part = count // 4
    copies = []
    for piece, out in enumerate(outs):
        for at, ref in enumerate((a, b, c, d)):
            rows = out.at[:, pl.ds(at * part, part), :]
            copies.append(load(ref.at[pl.ds(piece * size, size)], rows, sems.at[piece, at]))
    for copy in copies:
        copy.wait()


def products(lefts, parts, left_held, right_held, sems, outs):
    _, size, depth, _ = left_held.shape
    part = depth // 4
    row, col = lax.axis_index("row"), lax.axis_index("col")
    loads, start = [], 0
    for at in range(len(lefts) // 2):
        count = lefts[2 * at].shape[0]
        which = pl.ds(start, count)
        loads.append(load(lefts[2 * at], left_held.at[col, which], sems.at[len(loads)]))
        loads.append(load(lefts[2 * at + 1], left_held.at[1 - col, which], sems.at[len(loads)]))
        start += count
    for at, ref in enumerate(parts):
        loads.append(
            load(
                ref.at[pl.ds(size, size)],
                right_held.at[:, pl.ds(at * part, part), :],
                sems.at[len(loads)],
            )
        )
    low = (row < 4).astype(jnp.int32)
    for copy in loads:
        copy.wait()
    for side, held in ((low, outs[0]), (1 - low, outs[1])):
        for u in range(size):
            product = lax.dot_general(
                left_held[side, u], right_held[u], matmul_tn, preferred_element_type=jnp.float32
            )
            held[u] = product.astype(held.dtype)
        yield held


def contract_kernel(count, *refs):
    lefts, parts = refs[:count], refs[count : count + 4]
    away, keep, left_held, right_held, away_held, keep_held, sems = refs[count + 4 :]
    stores = []
    helds = (away_held, keep_held)
    for at, held in enumerate(products(lefts, parts, left_held, right_held, sems, helds)):
        stores.append(load(held, (away, keep)[at], sems.at[count + 4 + at]))
    for copy in stores:
        copy.wait()


def last_contract_kernel(count, *refs):
    lefts, parts = refs[:count], refs[count : count + 4]
    outs = refs[count + 4 : count + 8], refs[count + 8 : count + 12]
    left_held, right_held, away_held, keep_held, sems = refs[count + 12 :]
    part = left_held.shape[2] // 4
    row = lax.axis_index("row")
    stores = []
    helds = (away_held, keep_held)
    for half, held in enumerate(products(lefts, parts, left_held, right_held, sems, helds)):
        for slot, out in enumerate(outs[half]):
            rows = pl.ds(pl.multiple_of(((row % 4) ^ slot) * part, part), part)
            place = count + 4 + 4 * half + slot
            stores.append(load(held.at[:, rows, :], out, sems.at[place]))
    for copy in stores:
        copy.wait()


def add_kernel(keep, arrived, *refs):
    lasts, outs = refs[:4], refs[4:8]
    keep_held, arrived_held, sems = refs[8:]
    size, part = keep.shape[0], outs[0].shape[1]
    row = lax.axis_index("row")
    loads = [load(keep, keep_held, sems.at[0]), load(arrived, arrived_held, sems.at[1])]
    stores = [
        load(last, out.at[pl.ds(size, last.shape[0])], sems.at[2 + at])
        for at, (last, out) in enumerate(zip(lasts, outs, strict=True))
    ]
    for copy in loads:
        copy.wait()
    for u in range(size):
        total = keep_held[u] + arrived_held[u].astype(jnp.float32)
        arrived_held[u] = total.astype(jnp.bfloat16)
    for slot, out in enumerate(outs):
        rows = pl.ds(pl.multiple_of(((row % 4) ^ slot) * part, part), part)
        stores.append(
            load(arrived_held.at[:, rows, :], out.at[pl.ds(0, size)], sems.at[6 + slot])
        )
    for copy in stores:
        copy.wait()


def finish_kernel(rows, ranges, *refs):
    aways, totals = refs[:4], refs[4:8]
    opened, gain, bias, proj, out = refs[8:13]
    parts_held, last_held, opened_held, gain_held, bias_held, proj_held, out_held, sems = refs[13:]
    hidden, tile_rows, tile_cols = parts_held.shape
    last_start = ranges[-1][0]
    row = lax.axis_index("row")
    moves = [(gain, gain_held), (bias, bias_held), (proj, proj_held)]
    for slot in range(4):
        from_slot = (row % 4) ^ slot
        offset = 0
        for start, stop in ranges:
            size = (stop - start) // 4
            target = parts_held.at[pl.ds(start + from_slot * size, size)]
            moves.append((totals[slot].at[pl.ds(offset, size)], target))
            offset += size
        moves.append((aways[slot], last_held.at[pl.ds(from_slot * size, size)]))
    moves.append((opened, opened_held))
    loads = [load(source, target, sems.at[at]) for at, (source, target) in enumerate(moves)]
    for copy in loads[:-1]:
        copy.wait()
    gain_rows = jnp.broadcast_to(gain_held[...], (hidden, hidden)).T
    bias_rows = jnp.broadcast_to(bias_held[...], (hidden, hidden)).T
    zero = jnp.zeros((tile_rows, tile_cols), jnp.float32)

    def early(h):
        return parts_held[h].astype(jnp.float32)

    def late(h):
        return early(h) + last_held[h - last_start].astype(jnp.float32)

    def over_channels(step):
        done = lax.fori_loop(0, last_start, lambda h, s: s + step(early(h)), zero, unroll=8)
        done = lax.fori_loop(last_start, hidden, lambda h, s: s + step(late(h)), done, unroll=8)
        return done * (1.0 / hidden)

    average = over_channels(lambda value: value)
    spread = over_channels(lambda value: (value - average) * (value - average))
    scale = lax.rsqrt(spread + epsilon)
    stores = []
    loads[-1].wait()
    for b in range(tile_rows // rows):
        at = b * rows
        own = slice(at, at + rows)
        first = parts_held[:last_start, own, :].astype(jnp.float32)
        second = parts_held[last_start:, own, :].astype(jnp.float32)
        second = second + last_held[:, own, :].astype(jnp.float32)
        centered = jnp.concatenate([first, second], axis=0) - average[None, own]
        swapped = jnp.swapaxes(centered * scale[None, own], 0, 1)
        scaled = (swapped * gain_rows[None] + bias_rows[None]).astype(jnp.bfloat16)
        for step in range(rows):
            projected = lax.dot_general(
                scaled[step], proj_held[...], matmul_tn, preferred_element_type=jnp.float32
            )
            out_held[at + step] = (opened_held[at + step] * projected).astype(jnp.bfloat16)
        part = pl.ds(at, rows)
        stores.append(load(out_held.at[part], out.at[part], sems.at[len(moves) + b]))
    for copy in stores:
        copy.wait()


def shards_by_halves(
    pair,
    length,
    norm_in_gain,
    norm_in_bias,
    proj_in,
    gate_in,
    gate_out,
    norm_out_gain,
    norm_out_bias,
    proj_out,
):
    tile_rows, tile_cols, channels = pair.shape
    hidden = proj_out.shape[0]
    rows = lax.axis_size("row")
    block = min(16, tile_rows)
    blocks = tile_rows // block
    stops = [4 * sum(chunk_sizes[: at + 1]) for at in range(len(chunk_sizes))]
    ranges = list(zip([0, *stops[:-1]], stops, strict=True))
    wide = proj_in.shape[1]
    vmem, semaphores = pltpu.VMEM, pltpu.SemaphoreType.DMA
    small = jnp.bfloat16
    weights_scratch = [vmem(proj_in.shape, small), vmem(gate_in.shape, small)]
    turned = vmem((2 * wide, channels), small)
    depth = 4 * tile_rows

    def exchanged(value, mask):
        return lax.ppermute(value, "row", [(source, source ^ mask) for source in range(rows)])

    def edge_arrays(size):
        return [array((2 * size, tile_rows, tile_cols))] * 4

    def edge_scratch(size):
        return vmem((4, 2 * size, tile_rows, tile_cols), small)

    def edges_of(at, normed):
        return call(
            functools.partial(later_kernel, (*ranges[at], block)),
            edge_arrays(chunk_sizes[at]),
            [
                vmem(pair.shape, small),
                *weights_scratch,
                turned,
                edge_scratch(chunk_sizes[at]),
                semaphores((7,)),
            ],
            [in_smem] + [in_any] * 3,
            "later_edges",
        )(length, normed, proj_in, gate_in)

    def received(pieces):
        return [pieces[0], *[exchanged(pieces[mask], mask) for mask in (3, 2, 1)][::-1]]

    def swapped_left(at, after, pieces):
        size = chunk_sizes[at] // swap_pieces[at]
        lefts = call(
            pack_kernel,
            [array((size, depth, tile_cols))] * swap_pieces[at],
            [semaphores((swap_pieces[at], 4))],
            [in_any] * 5,
            "pack_left",
        )(after, *pieces)
        return [side for left in lefts for side in (left, from_partner(left, "col", 0))]

    def product_scratch(size, kept, count):
        shape = (size, depth, tile_cols)
        return [
            vmem((2, *shape), small),
            vmem(shape, small),
            vmem(shape, small),
            vmem(shape, kept),
            semaphores((count,)),
        ]

    def contracted(at, after, pieces):
        size = chunk_sizes[at]
        shape = (size, depth, tile_cols)
        lefts = swapped_left(at, after, pieces)
        return call(
            functools.partial(contract_kernel, len(lefts)),
            [array(shape), array(shape, jnp.float32)],
            product_scratch(size, jnp.float32, len(lefts) + 6),
            [in_any] * (len(lefts) + 4),
            "contract",
        )(*lefts, *pieces)

    def last_contracted(at, after, pieces):
        size = chunk_sizes[at]
        lefts = swapped_left(at, after, pieces)
        return call(
            functools.partial(last_contract_kernel, len(lefts)),
            [array((size, tile_rows, tile_cols))] * 8,
            product_scratch(size, small, len(lefts) + 12),
            [in_any] * (len(lefts) + 4),
            "contract",
        )(*lefts, *pieces)

    normed, *first = call(
        functools.partial(first_kernel, (*ranges[0], block)),
        [array(pair.shape), *edge_arrays(chunk_sizes[0])],
        [
            vmem(pair.shape, small),
            vmem((1, channels), jnp.float32),
            vmem((1, channels), jnp.float32),
            *weights_scratch,
            turned,
            vmem(pair.shape, small),
            edge_scratch(chunk_sizes[0]),
            semaphores((9 + blocks,)),
        ],
        [in_smem] + [in_any] * 5,
        "norm_and_first_edges",
        vmem_all,
    )(length, pair, norm_in_gain[None], norm_in_bias[None], proj_in, gate_in)
    first = received(first)
    second = edges_of(1, normed)
    away, keep = contracted(0, second[0], first)
    second = received(second)
    arrived = exchanged(away, 4)
    (opened,) = call(
        functools.partial(gate_kernel, block),
        [array(pair.shape, jnp.float32)],
        [
            vmem(pair.shape, small),
            vmem(gate_out.shape, small),
            vmem(pair.shape, jnp.float32),
            semaphores((2 + blocks,)),
        ],
        [in_any] * 3,
        "output_gate",
    )(away, normed, gate_out)
    last = last_contracted(1, opened, second)
    aways = [exchanged(last[mask], 4 ^ mask) for mask in range(4)]
    size = chunk_sizes[0]
    totals = call(
        add_kernel,
        [array((sum(chunk_sizes), tile_rows, tile_cols))] * 4,
        [
            vmem((size, depth, tile_cols), jnp.float32),
            vmem((size, depth, tile_cols), small),
            semaphores((10,)),
        ],
        [in_any] * 6,
        "add_halves",
    )(keep, arrived, *last[4:])
    totals = [totals[0], *[exchanged(totals[mask], mask) for mask in (1, 2, 3)]]
    (update,) = call(
        functools.partial(finish_kernel, 8, ranges),
        [array(pair.shape)],
        [
            vmem((hidden, tile_rows, tile_cols), small),
            vmem((4 * chunk_sizes[-1], tile_rows, tile_cols), small),
            vmem(pair.shape, jnp.float32),
            vmem((1, hidden), jnp.float32),
            vmem((1, hidden), jnp.float32),
            vmem(proj_out.shape, small),
            vmem(pair.shape, small),
            semaphores((4 + 4 * (len(ranges) + 1) + tile_rows // 8,)),
        ],
        [in_any] * 12,
        "norm_and_project_out",
    )(*aways, *totals, opened, norm_out_gain[None], norm_out_bias[None], proj_out)
    return update


def solution(mesh):
    placed = (P(("grp", "row"), "col", None), P("grp"), P(), P(), P(), P(), P(), P(), P(), P())
    return jax.shard_map(
        shards_by_halves if mesh.shape["row"] == 8 else shards_by_exchange,
        mesh=mesh,
        in_specs=placed,
        out_specs=P(("grp", "row"), "col", None),
        check_vma=False,
    )
```

```python
import functools

import jax
import jax.numpy as jnp
from jax import lax
from jax.experimental import pallas as pl
from jax.experimental.pallas import tpu as pltpu
from jax.sharding import PartitionSpec as P

epsilon = 1e-05
chunk_sizes = (12, 20)
swap_pieces = ((6, 6), (10, 10))
vmem_all = 60 * 1024 * 1024
vmem_part = 28 * 1024 * 1024


def from_partner(value, axis, apart):
    mask = 2**apart
    pairs = [(source, source ^ mask) for source in range(lax.axis_size(axis))]
    return lax.ppermute(value, axis, pairs)


def normalize_in(pair, gain, bias):
    widened = pair.astype(jnp.float32)
    average = jnp.mean(widened, axis=-1, keepdims=True)
    centered = widened - average
    spread = jnp.mean(centered * centered, axis=-1, keepdims=True)
    return (centered * lax.rsqrt(spread + epsilon) * gain + bias).astype(jnp.bfloat16)


def token_mask(tile_rows, tile_cols, length):
    row_start = lax.axis_index("row") * tile_rows
    col_start = lax.axis_index("col") * tile_cols
    valid_rows = row_start + jnp.arange(tile_rows, dtype=jnp.int32) < length[0]
    valid_cols = col_start + jnp.arange(tile_cols, dtype=jnp.int32) < length[0]
    return (valid_rows[:, None] & valid_cols[None, :]).astype(jnp.float32)


def make_edges(normed, proj, gate, mask):
    projected = jnp.einsum("ijc,ch->hij", normed, proj, preferred_element_type=jnp.float32)
    gating = jnp.einsum("ijc,ch->hij", normed, gate, preferred_element_type=jnp.float32)
    return (jax.nn.sigmoid(gating) * projected * mask[None]).astype(jnp.bfloat16)


def finish(contracted, normed, gate_out, gain, bias, proj_out):
    widened = contracted.astype(jnp.float32)
    average = jnp.mean(widened, axis=0, keepdims=True)
    centered = widened - average
    spread = jnp.mean(centered * centered, axis=0, keepdims=True)
    scaled = centered * lax.rsqrt(spread + epsilon) * gain[:, None, None]
    contracted_norm = (scaled + bias[:, None, None]).astype(jnp.bfloat16)
    out_gate = jax.nn.sigmoid(
        jnp.einsum("ijc,cd->ijd", normed, gate_out, preferred_element_type=jnp.float32)
    )
    projected_out = jnp.einsum(
        "hij,hc->ijc", contracted_norm, proj_out, preferred_element_type=jnp.float32
    )
    return (out_gate * projected_out).astype(jnp.bfloat16)


def contract(left, right):
    return jnp.einsum("hki,hkj->hij", left, right, preferred_element_type=jnp.float32)


def shards_by_exchange(
    pair,
    length,
    norm_in_gain,
    norm_in_bias,
    proj_in,
    gate_in,
    gate_out,
    norm_out_gain,
    norm_out_bias,
    proj_out,
):
    hidden = proj_out.shape[0]
    normed = normalize_in(pair, norm_in_gain, norm_in_bias)
    mask = token_mask(pair.shape[0], pair.shape[1], length)
    edges = make_edges(normed, proj_in, gate_in, mask)
    left_rows = lax.all_to_all(edges[:hidden], "row", split_axis=0, concat_axis=1, tiled=True)
    right_rows = lax.all_to_all(edges[hidden:], "row", split_axis=0, concat_axis=1, tiled=True)
    other_half = from_partner(left_rows, "col", 0)
    first_col = lax.axis_index("col") == 0
    left_full = jnp.where(
        first_col,
        jnp.concatenate([left_rows, other_half], axis=2),
        jnp.concatenate([other_half, left_rows], axis=2),
    )
    contracted = contract(left_full, right_rows).astype(jnp.bfloat16)
    returned = lax.all_to_all(contracted, "row", split_axis=1, concat_axis=0, tiled=True)
    return finish(returned, normed, gate_out, norm_out_gain, norm_out_bias, proj_out)


in_smem = pl.BlockSpec(memory_space=pltpu.SMEM)
in_any = pl.BlockSpec(memory_space=pl.ANY)
in_vmem = pl.BlockSpec(memory_space=pltpu.VMEM)
matmul_tn = (((0,), (0,)), ((), ()))
matmul_nt = (((1,), (1,)), ((), ()))


def call(kernel, outputs, scratch, specs, out_specs, name, limit=vmem_part):
    return pl.pallas_call(
        kernel,
        out_shape=outputs,
        in_specs=specs,
        out_specs=out_specs,
        scratch_shapes=scratch,
        compiler_params=pltpu.CompilerParams(vmem_limit_bytes=limit),
        name=name,
    )


def array(shape, dtype=jnp.bfloat16):
    return jax.ShapeDtypeStruct(shape, dtype)


def load(source, target, sem):
    copy = pltpu.make_async_copy(source, target, sem)
    copy.start()
    return copy


def chosen_weights(start, size, slots, row, proj, gate):
    width = proj.shape[1]
    first_slot, slot_count = slots
    count = 2 * slot_count * size
    at = lax.broadcasted_iota(jnp.int32, (count, width), 0)
    side, inside = at // (slot_count * size), at % (slot_count * size)
    slot, channel = first_slot + inside // size, inside % size
    source = side * (width // 2) + start + ((row % 4) ^ slot) * size + channel
    one_hot = (lax.broadcasted_iota(jnp.int32, (count, width), 1) == source).astype(jnp.bfloat16)
    picked = [
        lax.dot_general(one_hot, weights, matmul_nt, preferred_element_type=jnp.float32)
        for weights in (proj, gate)
    ]
    return jnp.concatenate(picked, axis=0).astype(jnp.bfloat16)


def block_edges(length, normed, weights, at, row_start, col_start, outs):
    rows, tile_cols, channels = normed.shape
    size = outs[0].shape[0] // 2
    pairs = lax.dot_general(
        weights,
        normed.reshape(rows * tile_cols, channels),
        matmul_nt,
        preferred_element_type=jnp.float32,
    )
    count = pairs.shape[0] // 2
    values = jax.nn.sigmoid(pairs[count:]) * pairs[:count]
    cols = col_start + lax.broadcasted_iota(jnp.int32, (count, tile_cols), 1)
    masked = []
    for row in range(rows):
        limit = jnp.where(row_start + at + row < length, length, 0)
        piece = values[:, row * tile_cols : (row + 1) * tile_cols]
        masked.append(jnp.where(cols < limit, piece, 0.0))
    swapped = jnp.swapaxes(jnp.stack(masked, axis=0), 0, 1).astype(jnp.bfloat16)
    for slot, out in enumerate(outs):
        for side in range(2):
            first = (side * len(outs) + slot) * size
            out[side * size : (side + 1) * size, at : at + rows, :] = swapped[first : first + size]


def first_kernel(bounds, length, pair, gain, bias, proj, gate, normed, *rest):
    start, size, rows = bounds
    outs = rest[:3]
    pair_held, gain_held, bias_held, proj_held, gate_held, normed_held = rest[3:9]
    helds, sems = rest[9:12], rest[12]
    tile_rows, tile_cols, channels = pair.shape
    blocks = tile_rows // rows
    parts = [pl.ds(b * rows, rows) for b in range(blocks)]
    pieces = [load(pair.at[p], pair_held.at[p], sems.at[b, 0]) for b, p in enumerate(parts)]
    small = [
        load(source, target, sems.at[blocks, at])
        for at, (source, target) in enumerate(
            ((proj, proj_held), (gate, gate_held), (gain, gain_held), (bias, bias_held))
        )
    ]
    row = lax.axis_index("row")
    row_start = row * tile_rows
    col_start = lax.axis_index("col") * tile_cols
    for copy in small:
        copy.wait()
    weights = chosen_weights(start, size, (1, 3), row, proj_held[...], gate_held[...])
    mean = jnp.full((channels, channels), 1.0 / channels, jnp.bfloat16)
    stores = []
    for b, part in enumerate(parts):
        at = b * rows
        pieces[b].wait()
        tokens = pair_held[at : at + rows].reshape(rows * tile_cols, channels)
        average = jnp.dot(tokens, mean, preferred_element_type=jnp.float32)
        centered = tokens.astype(jnp.float32) - average
        spread = jnp.mean(centered * centered, axis=-1, keepdims=True)
        scaled = centered * lax.rsqrt(spread + epsilon) * gain_held[...] + bias_held[...]
        rounded = scaled.astype(jnp.bfloat16).reshape(rows, tile_cols, channels)
        normed_held[at : at + rows] = rounded
        stores.append(load(normed_held.at[part], normed.at[part], sems.at[b, 1]))
        block_edges(length[0], rounded, weights, at, row_start, col_start, helds)
        for slot, out in enumerate(outs):
            stores.append(load(helds[slot].at[:, part], out.at[:, part], sems.at[b, 2 + slot]))
    for copy in stores:
        copy.wait()


def later_kernel(bounds, length, normed, proj, gate, *outs):
    rows, *chunks = bounds
    tile_rows, tile_cols, _ = normed.shape
    row = lax.axis_index("row")
    row_start = row * tile_rows
    col_start = lax.axis_index("col") * tile_cols
    for start, size, slots in chunks:
        weights = chosen_weights(start, size, slots, row, proj[...], gate[...])
        for at in range(0, tile_rows, rows):
            tokens = normed[at : at + rows]
            targets = outs[: slots[1]]
            block_edges(length[0], tokens, weights, at, row_start, col_start, targets)
        outs = outs[slots[1] :]


def gate_kernel(rows, after, normed, weights, out):
    tile_rows, tile_cols, channels = normed.shape
    for at in range(0, tile_rows, rows):
        gating = jnp.dot(
            normed[at : at + rows].reshape(rows * tile_cols, channels),
            weights[...],
            preferred_element_type=jnp.float32,
        )
        out[at : at + rows] = jax.nn.sigmoid(gating).reshape(rows, tile_cols, channels)


def pack_kernel(after, a, b, c, d, *rest):
    outs, sems = rest[:-1], rest[-1]
    copies, start = [], 0
    for piece, out in enumerate(outs):
        size, count, _ = out.shape
        part = count // 4
        for at, ref in enumerate((a, b, c, d)):
            rows = out.at[:, pl.ds(at * part, part), :]
            copies.append(load(ref.at[pl.ds(start, size)], rows, sems.at[piece, at]))
        start += size
    for copy in copies:
        copy.wait()


def contractions(lefts, parts, store):
    size = parts[0].shape[0] // 2
    places = [(at, u) for at in range(0, len(lefts), 2) for u in range(lefts[at].shape[0])]
    low = lax.axis_index("row") < 4
    own_away = (lax.axis_index("col") == 1) == low

    def both(first):
        for u in range(size):
            right = jnp.concatenate([part[size + u] for part in parts], axis=0)
            for side in range(2):
                left = lefts[places[u][0] + (first ^ side)][places[u][1]]
                product = lax.dot_general(
                    left, right, matmul_tn, preferred_element_type=jnp.float32
                )
                store(u, side, product)

    pl.when(own_away)(functools.partial(both, 0))
    pl.when(jnp.logical_not(own_away))(functools.partial(both, 1))


def contract_kernel(count, *refs):
    lefts, parts = refs[:count], refs[count : count + 4]
    outs = refs[count + 4 :]

    def store(u, side, product):
        outs[side][u] = product.astype(outs[side].dtype)

    contractions(lefts, parts, store)


def last_contract_kernel(count, *refs):
    lefts, parts = refs[:count], refs[count : count + 4]
    outs = refs[count + 4 : count + 8], refs[count + 8 : count + 12]
    held = refs[count + 12]
    part = outs[0][0].shape[1]
    row = lax.axis_index("row")

    def store(u, side, product):
        held[u, side] = product.astype(jnp.bfloat16)
        for slot, out in enumerate(outs[side]):
            rows = pl.ds(pl.multiple_of(((row % 4) ^ slot) * part, part), part)
            out[u] = held[u, side, rows, :]

    contractions(lefts, parts, store)


def add_kernel(keep, arrived, *refs):
    lasts, outs = refs[:4], refs[4:8]
    keep_held, arrived_held, sems = refs[8:]
    size, part = keep.shape[0], outs[0].shape[1]
    row = lax.axis_index("row")
    loads = [load(keep, keep_held, sems.at[0]), load(arrived, arrived_held, sems.at[1])]
    stores = [
        load(last, out.at[pl.ds(size, last.shape[0])], sems.at[2 + at])
        for at, (last, out) in enumerate(zip(lasts, outs, strict=True))
    ]
    for copy in loads:
        copy.wait()
    for u in range(size):
        total = keep_held[u] + arrived_held[u].astype(jnp.float32)
        arrived_held[u] = total.astype(jnp.bfloat16)
    for slot, out in enumerate(outs):
        rows = pl.ds(pl.multiple_of(((row % 4) ^ slot) * part, part), part)
        stores.append(
            load(arrived_held.at[:, rows, :], out.at[pl.ds(0, size)], sems.at[6 + slot])
        )
    for copy in stores:
        copy.wait()


def finish_kernel(rows, sizes, *refs):
    aways, totals = refs[:4], refs[4:8]
    opened, gain, bias, proj, out, out_held, sems = refs[8:]
    early, late = sizes
    tile_rows = out.shape[0]
    hidden, per = proj.shape[0], early + late
    row = lax.axis_index("row")
    at = lax.broadcasted_iota(jnp.int32, (hidden, hidden), 0)
    slot, place = at // per, at % per
    owner = (row % 4) ^ slot
    channel = jnp.where(
        place < early, owner * early + place, 4 * early + owner * late + place - early
    )
    picked = lax.broadcasted_iota(jnp.int32, (hidden, hidden), 1) == channel

    def down(values):
        column = jnp.sum(jnp.where(picked, values, 0.0), axis=1, keepdims=True)
        return jnp.broadcast_to(column, (hidden, hidden))[None]

    gain_rows, bias_rows = down(gain[...]), down(bias[...])
    ordered = jnp.dot(
        picked.astype(jnp.bfloat16), proj[...], preferred_element_type=jnp.float32
    ).astype(jnp.bfloat16)
    stores = []
    for b in range(tile_rows // rows):
        own = slice(b * rows, (b + 1) * rows)
        pieces = []
        for total, away in zip(totals, aways, strict=True):
            pieces.append(total[:early, own, :].astype(jnp.float32))
            kept = total[early:, own, :].astype(jnp.float32)
            pieces.append(kept + away[:, own, :].astype(jnp.float32))
        values = jnp.concatenate(pieces, axis=0)
        centered = values - jnp.sum(values, axis=0, keepdims=True) * (1.0 / hidden)
        spread = jnp.sum(centered * centered, axis=0, keepdims=True) * (1.0 / hidden)
        swapped = jnp.swapaxes(centered * lax.rsqrt(spread + epsilon), 0, 1)
        scaled = (swapped * gain_rows + bias_rows).astype(jnp.bfloat16)
        for step in range(rows):
            projected = lax.dot_general(
                scaled[step], ordered, matmul_tn, preferred_element_type=jnp.float32
            )
            at_row = b * rows + step
            out_held[at_row] = (opened[at_row] * projected).astype(jnp.bfloat16)
        part = pl.ds(b * rows, rows)
        stores.append(load(out_held.at[part], out.at[part], sems.at[b]))
    for copy in stores:
        copy.wait()


def shards_by_halves(
    pair,
    length,
    norm_in_gain,
    norm_in_bias,
    proj_in,
    gate_in,
    gate_out,
    norm_out_gain,
    norm_out_bias,
    proj_out,
):
    tile_rows, tile_cols, channels = pair.shape
    rows = lax.axis_size("row")
    block = min(16, tile_rows)
    blocks = tile_rows // block
    early, late = chunk_sizes
    vmem, semaphores = pltpu.VMEM, pltpu.SemaphoreType.DMA
    small = jnp.bfloat16
    depth = 4 * tile_rows

    def exchanged(value, mask):
        return lax.ppermute(value, "row", [(source, source ^ mask) for source in range(rows)])

    def edge_shape(size):
        return (2 * size, tile_rows, tile_cols)

    def received(pieces):
        return [pieces[0], *[exchanged(pieces[mask], mask) for mask in (3, 2, 1)]]

    def swapped_left(at, after, pieces):
        sizes = swap_pieces[at]
        lefts = call(
            pack_kernel,
            [array((size, depth, tile_cols)) for size in sizes],
            [semaphores((len(sizes), 4))],
            [in_any] * 5,
            [in_any] * len(sizes),
            "pack_left",
        )(after, *pieces)
        return [side for left in lefts for side in (left, from_partner(left, "col", 0))]

    normed, *sent = call(
        functools.partial(first_kernel, (0, early, block)),
        [array(pair.shape), *[array(edge_shape(early))] * 3],
        [
            vmem(pair.shape, small),
            vmem((1, channels), jnp.float32),
            vmem((1, channels), jnp.float32),
            vmem(proj_in.shape, small),
            vmem(gate_in.shape, small),
            vmem(pair.shape, small),
            *[vmem(edge_shape(early), small)] * 3,
            semaphores((blocks + 1, 5)),
        ],
        [in_smem] + [in_any] * 5,
        [in_any] * 4,
        "norm_and_first_edges",
        vmem_all,
    )(length, pair, norm_in_gain[None], norm_in_bias[None], proj_in, gate_in)
    own, *second = call(
        functools.partial(later_kernel, (block, (0, early, (0, 1)), (4 * early, late, (0, 4)))),
        [array(edge_shape(early)), *[array(edge_shape(late))] * 4],
        [],
        [in_smem] + [in_vmem] * 3,
        [in_vmem] * 5,
        "later_edges",
    )(length, normed, proj_in, gate_in)
    first = received([own, *sent])
    lefts = swapped_left(0, second[0], first)
    shape = (early, depth, tile_cols)
    away, keep = call(
        functools.partial(contract_kernel, len(lefts)),
        [array(shape), array(shape, jnp.float32)],
        [],
        [in_vmem] * (len(lefts) + 4),
        [in_vmem] * 2,
        "contract",
    )(*lefts, *first)
    arrived = exchanged(away, 4)
    second = received(second)
    (opened,) = call(
        functools.partial(gate_kernel, block),
        [array(pair.shape, jnp.float32)],
        [],
        [in_any] + [in_vmem] * 2,
        [in_vmem],
        "output_gate",
    )(away, normed, gate_out)
    lefts = swapped_left(1, opened, second)
    last = call(
        functools.partial(last_contract_kernel, len(lefts)),
        [array((late, tile_rows, tile_cols))] * 8,
        [vmem((late, 2, depth, tile_cols), small)],
        [in_vmem] * (len(lefts) + 4),
        [in_vmem] * 8,
        "contract",
    )(*lefts, *second)
    aways = [exchanged(last[mask], 4 ^ mask) for mask in range(4)]
    totals = call(
        add_kernel,
        [array((early + late, tile_rows, tile_cols))] * 4,
        [
            vmem((early, depth, tile_cols), jnp.float32),
            vmem((early, depth, tile_cols), small),
            semaphores((10,)),
        ],
        [in_any] * 6,
        [in_any] * 4,
        "add_halves",
    )(keep, arrived, *last[4:])
    totals = [totals[0], *[exchanged(totals[mask], mask) for mask in (1, 2, 3)]]
    (update,) = call(
        functools.partial(finish_kernel, 8, chunk_sizes),
        [array(pair.shape)],
        [vmem(pair.shape, small), semaphores((tile_rows // 8,))],
        [in_vmem] * 12,
        [in_any],
        "norm_and_project_out",
    )(*aways, *totals, opened, norm_out_gain[None], norm_out_bias[None], proj_out)
    return update


def solution(mesh):
    placed = (P(("grp", "row"), "col", None), P("grp"), P(), P(), P(), P(), P(), P(), P(), P())
    return jax.shard_map(
        shards_by_halves if mesh.shape["row"] == 8 else shards_by_exchange,
        mesh=mesh,
        in_specs=placed,
        out_specs=P(("grp", "row"), "col", None),
        check_vma=False,
    )
```

```python
import functools

import jax
import jax.numpy as jnp
from jax import lax
from jax.experimental import pallas as pl
from jax.experimental.pallas import tpu as pltpu
from jax.sharding import PartitionSpec as P

epsilon = 1e-05
chunk_sizes = (13, 19)
vmem_all = 60 * 1024 * 1024
vmem_part = 28 * 1024 * 1024


def from_partner(value, axis, apart):
    mask = 2**apart
    pairs = [(source, source ^ mask) for source in range(lax.axis_size(axis))]
    return lax.ppermute(value, axis, pairs)


def normalize_in(pair, gain, bias):
    widened = pair.astype(jnp.float32)
    average = jnp.mean(widened, axis=-1, keepdims=True)
    centered = widened - average
    spread = jnp.mean(centered * centered, axis=-1, keepdims=True)
    return (centered * lax.rsqrt(spread + epsilon) * gain + bias).astype(jnp.bfloat16)


def token_mask(tile_rows, tile_cols, length):
    row_start = lax.axis_index("row") * tile_rows
    col_start = lax.axis_index("col") * tile_cols
    valid_rows = row_start + jnp.arange(tile_rows, dtype=jnp.int32) < length[0]
    valid_cols = col_start + jnp.arange(tile_cols, dtype=jnp.int32) < length[0]
    return (valid_rows[:, None] & valid_cols[None, :]).astype(jnp.float32)


def make_edges(normed, proj, gate, mask):
    projected = jnp.einsum("ijc,ch->hij", normed, proj, preferred_element_type=jnp.float32)
    gating = jnp.einsum("ijc,ch->hij", normed, gate, preferred_element_type=jnp.float32)
    return (jax.nn.sigmoid(gating) * projected * mask[None]).astype(jnp.bfloat16)


def finish(contracted, normed, gate_out, gain, bias, proj_out):
    widened = contracted.astype(jnp.float32)
    average = jnp.mean(widened, axis=0, keepdims=True)
    centered = widened - average
    spread = jnp.mean(centered * centered, axis=0, keepdims=True)
    scaled = centered * lax.rsqrt(spread + epsilon) * gain[:, None, None]
    contracted_norm = (scaled + bias[:, None, None]).astype(jnp.bfloat16)
    out_gate = jax.nn.sigmoid(
        jnp.einsum("ijc,cd->ijd", normed, gate_out, preferred_element_type=jnp.float32)
    )
    projected_out = jnp.einsum(
        "hij,hc->ijc", contracted_norm, proj_out, preferred_element_type=jnp.float32
    )
    return (out_gate * projected_out).astype(jnp.bfloat16)


def contract(left, right):
    return jnp.einsum("hki,hkj->hij", left, right, preferred_element_type=jnp.float32)


def shards_by_exchange(
    pair,
    length,
    norm_in_gain,
    norm_in_bias,
    proj_in,
    gate_in,
    gate_out,
    norm_out_gain,
    norm_out_bias,
    proj_out,
):
    hidden = proj_out.shape[0]
    normed = normalize_in(pair, norm_in_gain, norm_in_bias)
    mask = token_mask(pair.shape[0], pair.shape[1], length)
    edges = make_edges(normed, proj_in, gate_in, mask)
    left_rows = lax.all_to_all(edges[:hidden], "row", split_axis=0, concat_axis=1, tiled=True)
    right_rows = lax.all_to_all(edges[hidden:], "row", split_axis=0, concat_axis=1, tiled=True)
    other_half = from_partner(left_rows, "col", 0)
    first_col = lax.axis_index("col") == 0
    left_full = jnp.where(
        first_col,
        jnp.concatenate([left_rows, other_half], axis=2),
        jnp.concatenate([other_half, left_rows], axis=2),
    )
    contracted = contract(left_full, right_rows).astype(jnp.bfloat16)
    returned = lax.all_to_all(contracted, "row", split_axis=1, concat_axis=0, tiled=True)
    return finish(returned, normed, gate_out, norm_out_gain, norm_out_bias, proj_out)


in_smem = pl.BlockSpec(memory_space=pltpu.SMEM)
in_any = pl.BlockSpec(memory_space=pl.ANY)
in_vmem = pl.BlockSpec(memory_space=pltpu.VMEM)
matmul_tn = (((0,), (0,)), ((), ()))
matmul_nt = (((1,), (1,)), ((), ()))


def call(kernel, outputs, scratch, specs, out_specs, name, limit=vmem_part):
    return pl.pallas_call(
        kernel,
        out_shape=outputs,
        in_specs=specs,
        out_specs=out_specs,
        scratch_shapes=scratch,
        compiler_params=pltpu.CompilerParams(vmem_limit_bytes=limit),
        name=name,
    )


def array(shape, dtype=jnp.bfloat16):
    return jax.ShapeDtypeStruct(shape, dtype)


def load(source, target, sem):
    copy = pltpu.make_async_copy(source, target, sem)
    copy.start()
    return copy


def chosen_weights(start, size, slots, row, proj, gate):
    width = proj.shape[1]
    first_slot, slot_count = slots
    count = 2 * slot_count * size
    at = lax.broadcasted_iota(jnp.int32, (count, width), 0)
    side, inside = at // (slot_count * size), at % (slot_count * size)
    slot, channel = first_slot + inside // size, inside % size
    source = side * (width // 2) + start + ((row % 4) ^ slot) * size + channel
    one_hot = (lax.broadcasted_iota(jnp.int32, (count, width), 1) == source).astype(jnp.bfloat16)
    picked = [
        lax.dot_general(one_hot, weights, matmul_nt, preferred_element_type=jnp.float32)
        for weights in (proj, gate)
    ]
    return jnp.concatenate(picked, axis=0).astype(jnp.bfloat16)


def block_edges(length, normed, weights, at, row_start, col_start, outs):
    rows, tile_cols, channels = normed.shape
    size = outs[0].shape[0] // 2
    pairs = lax.dot_general(
        weights,
        normed.reshape(rows * tile_cols, channels),
        matmul_nt,
        preferred_element_type=jnp.float32,
    )
    count = pairs.shape[0] // 2
    values = jax.nn.sigmoid(pairs[count:]) * pairs[:count]
    cols = col_start + lax.broadcasted_iota(jnp.int32, (count, tile_cols), 1)
    masked = []
    for row in range(rows):
        limit = jnp.where(row_start + at + row < length, length, 0)
        piece = values[:, row * tile_cols : (row + 1) * tile_cols]
        masked.append(jnp.where(cols < limit, piece, 0.0))
    swapped = jnp.swapaxes(jnp.stack(masked, axis=0), 0, 1).astype(jnp.bfloat16)
    for slot, out in enumerate(outs):
        for side in range(2):
            first = (side * len(outs) + slot) * size
            out[side * size : (side + 1) * size, at : at + rows, :] = swapped[first : first + size]


def first_kernel(bounds, length, pair, gain, bias, proj, gate, normed, *rest):
    start, size, rows = bounds
    outs = rest[:3]
    pair_held, gain_held, bias_held, proj_held, gate_held, normed_held = rest[3:9]
    helds, sems = rest[9:12], rest[12]
    tile_rows, tile_cols, channels = pair.shape
    blocks = tile_rows // rows
    parts = [pl.ds(b * rows, rows) for b in range(blocks)]
    pieces = [load(pair.at[p], pair_held.at[p], sems.at[b, 0]) for b, p in enumerate(parts)]
    small = [
        load(source, target, sems.at[blocks, at])
        for at, (source, target) in enumerate(
            ((proj, proj_held), (gate, gate_held), (gain, gain_held), (bias, bias_held))
        )
    ]
    row = lax.axis_index("row")
    row_start = row * tile_rows
    col_start = lax.axis_index("col") * tile_cols
    for copy in small:
        copy.wait()
    weights = chosen_weights(start, size, (1, 3), row, proj_held[...], gate_held[...])
    mean = jnp.full((channels, channels), 1.0 / channels, jnp.bfloat16)
    stores = []
    for b, part in enumerate(parts):
        at = b * rows
        pieces[b].wait()
        tokens = pair_held[at : at + rows].reshape(rows * tile_cols, channels)
        average = jnp.dot(tokens, mean, preferred_element_type=jnp.float32)
        centered = tokens.astype(jnp.float32) - average
        spread = jnp.mean(centered * centered, axis=-1, keepdims=True)
        scaled = centered * lax.rsqrt(spread + epsilon) * gain_held[...] + bias_held[...]
        rounded = scaled.astype(jnp.bfloat16).reshape(rows, tile_cols, channels)
        normed_held[at : at + rows] = rounded
        stores.append(load(normed_held.at[part], normed.at[part], sems.at[b, 1]))
        block_edges(length[0], rounded, weights, at, row_start, col_start, helds)
        for slot, out in enumerate(outs):
            stores.append(load(helds[slot].at[:, part], out.at[:, part], sems.at[b, 2 + slot]))
    for copy in stores:
        copy.wait()


def later_kernel(bounds, length, normed, proj, gate, *outs):
    rows, *chunks = bounds
    tile_rows, tile_cols, _ = normed.shape
    row = lax.axis_index("row")
    row_start = row * tile_rows
    col_start = lax.axis_index("col") * tile_cols
    for start, size, slots in chunks:
        weights = chosen_weights(start, size, slots, row, proj[...], gate[...])
        for at in range(0, tile_rows, rows):
            tokens = normed[at : at + rows]
            targets = outs[: slots[1]]
            block_edges(length[0], tokens, weights, at, row_start, col_start, targets)
        outs = outs[slots[1] :]


def gate_kernel(rows, after, normed, weights, out):
    tile_rows, tile_cols, channels = normed.shape
    for at in range(0, tile_rows, rows):
        gating = jnp.dot(
            normed[at : at + rows].reshape(rows * tile_cols, channels),
            weights[...],
            preferred_element_type=jnp.float32,
        )
        out[at : at + rows] = jax.nn.sigmoid(gating).reshape(rows, tile_cols, channels)


def pack_kernel(after, a, b, out, sems):
    size, count, _ = out.shape
    part = count // 2
    copies = [
        load(ref.at[pl.ds(0, size)], out.at[:, pl.ds(at * part, part), :], sems.at[at])
        for at, ref in enumerate((a, b))
    ]
    for copy in copies:
        copy.wait()


def contractions(partners, parts, store):
    size = parts[0].shape[0] // 2
    low = lax.axis_index("row") < 4
    own_away = (lax.axis_index("col") == 1) == low

    def both(first):
        for u in range(size):
            right = jnp.concatenate([part[size + u] for part in parts], axis=0)
            own = jnp.concatenate([part[u] for part in parts], axis=0)
            theirs = jnp.concatenate([partner[u] for partner in partners], axis=0)
            for side in range(2):
                left = theirs if first ^ side else own
                product = lax.dot_general(
                    left, right, matmul_tn, preferred_element_type=jnp.float32
                )
                store(u, side, product)

    pl.when(own_away)(functools.partial(both, 0))
    pl.when(jnp.logical_not(own_away))(functools.partial(both, 1))


def contract_kernel(*refs):
    partners, parts, outs = refs[:2], refs[2:6], refs[6:]

    def store(u, side, product):
        outs[side][u] = product.astype(outs[side].dtype)

    contractions(partners, parts, store)


def last_contract_kernel(*refs):
    partners, parts = refs[:2], refs[2:6]
    outs, held = (refs[6:10], refs[10:14]), refs[14]
    part = outs[0][0].shape[1]
    row = lax.axis_index("row")

    def store(u, side, product):
        held[u, side] = product.astype(jnp.bfloat16)
        for slot, out in enumerate(outs[side]):
            rows = pl.ds(pl.multiple_of(((row % 4) ^ slot) * part, part), part)
            out[u] = held[u, side, rows, :]

    contractions(partners, parts, store)


def add_kernel(keep, arrived, *refs):
    lasts, outs, held = refs[:4], refs[4:8], refs[8]
    size, part = keep.shape[0], outs[0].shape[1]
    row = lax.axis_index("row")
    held[...] = (keep[...] + arrived[...].astype(jnp.float32)).astype(jnp.bfloat16)
    for slot, (last, out) in enumerate(zip(lasts, outs, strict=True)):
        rows = pl.ds(pl.multiple_of(((row % 4) ^ slot) * part, part), part)
        out[:size] = held[:, rows, :]
        out[size:] = last[...]


def finish_kernel(rows, sizes, *refs):
    aways, totals = refs[:4], refs[4:8]
    opened, gain, bias, proj, out, out_held, sems = refs[8:]
    early, late = sizes
    tile_rows = out.shape[0]
    hidden, per = proj.shape[0], early + late
    row = lax.axis_index("row")
    at = lax.broadcasted_iota(jnp.int32, (hidden, hidden), 0)
    slot, place = at // per, at % per
    owner = (row % 4) ^ ((4 - slot) % 4)
    channel = jnp.where(
        place < early, owner * early + place, 4 * early + owner * late + place - early
    )
    picked = lax.broadcasted_iota(jnp.int32, (hidden, hidden), 1) == channel

    def down(values):
        column = jnp.sum(jnp.where(picked, values, 0.0), axis=1, keepdims=True)
        return jnp.broadcast_to(column, (hidden, hidden))[None]

    gain_rows, bias_rows = down(gain[...]), down(bias[...])
    ordered = jnp.dot(
        picked.astype(jnp.bfloat16), proj[...], preferred_element_type=jnp.float32
    ).astype(jnp.bfloat16)
    stores = []
    for b in range(tile_rows // rows):
        own = slice(b * rows, (b + 1) * rows)
        pieces = []
        for total, away in zip(totals, aways, strict=True):
            pieces.append(total[:early, own, :].astype(jnp.float32))
            kept = total[early:, own, :].astype(jnp.float32)
            pieces.append(kept + away[:, own, :].astype(jnp.float32))
        values = jnp.concatenate(pieces, axis=0)
        centered = values - jnp.sum(values, axis=0, keepdims=True) * (1.0 / hidden)
        spread = jnp.sum(centered * centered, axis=0, keepdims=True) * (1.0 / hidden)
        swapped = jnp.swapaxes(centered * lax.rsqrt(spread + epsilon), 0, 1)
        scaled = (swapped * gain_rows + bias_rows).astype(jnp.bfloat16)
        for step in range(rows):
            projected = lax.dot_general(
                scaled[step], ordered, matmul_tn, preferred_element_type=jnp.float32
            )
            at_row = b * rows + step
            out_held[at_row] = (opened[at_row] * projected).astype(jnp.bfloat16)
        part = pl.ds(b * rows, rows)
        stores.append(load(out_held.at[part], out.at[part], sems.at[b]))
    for copy in stores:
        copy.wait()


def shards_by_halves(
    pair,
    length,
    norm_in_gain,
    norm_in_bias,
    proj_in,
    gate_in,
    gate_out,
    norm_out_gain,
    norm_out_bias,
    proj_out,
):
    tile_rows, tile_cols, channels = pair.shape
    rows = lax.axis_size("row")
    block = min(16, tile_rows)
    blocks = tile_rows // block
    early, late = chunk_sizes
    vmem, semaphores = pltpu.VMEM, pltpu.SemaphoreType.DMA
    small = jnp.bfloat16
    depth = 4 * tile_rows

    def exchanged(value, mask):
        return lax.ppermute(value, "row", [(source, source ^ mask) for source in range(rows)])

    def edge_shape(size):
        return (2 * size, tile_rows, tile_cols)

    def spread(pieces):
        return [pieces[0], *[exchanged(pieces[mask], mask) for mask in (3, 2, 1)]]

    def swapped_left(after, a, b):
        (left,) = call(
            pack_kernel,
            [array((a.shape[0] // 2, depth // 2, tile_cols))],
            [semaphores((2,))],
            [in_any] * 3,
            [in_any],
            "pack_left",
        )(after, a, b)
        return from_partner(left, "col", 0)

    normed, *sent = call(
        functools.partial(first_kernel, (0, early, block)),
        [array(pair.shape), *[array(edge_shape(early))] * 3],
        [
            vmem(pair.shape, small),
            vmem((1, channels), jnp.float32),
            vmem((1, channels), jnp.float32),
            vmem(proj_in.shape, small),
            vmem(gate_in.shape, small),
            vmem(pair.shape, small),
            *[vmem(edge_shape(early), small)] * 3,
            semaphores((blocks + 1, 5)),
        ],
        [in_smem] + [in_any] * 5,
        [in_any] * 4,
        "norm_and_first_edges",
        vmem_all,
    )(length, pair, norm_in_gain[None], norm_in_bias[None], proj_in, gate_in)
    own, *second = call(
        functools.partial(later_kernel, (block, (0, early, (0, 1)), (4 * early, late, (0, 4)))),
        [array(edge_shape(early)), *[array(edge_shape(late))] * 4],
        [],
        [in_smem] + [in_vmem] * 3,
        [in_vmem] * 5,
        "later_edges",
    )(length, normed, proj_in, gate_in)
    first = spread([own, *sent])
    partners = [swapped_left(second[0], first[0], first[3]), swapped_left(second[0], first[1], first[2])]
    parts = [first[0], first[3], first[1], first[2]]
    shape = (early, depth, tile_cols)
    away, keep = call(
        contract_kernel,
        [array(shape), array(shape, jnp.float32)],
        [],
        [in_vmem] * 6,
        [in_vmem] * 2,
        "contract",
    )(*partners, *parts)
    arrived = exchanged(away, 4)
    second = spread(second)
    (opened,) = call(
        functools.partial(gate_kernel, block),
        [array(pair.shape, jnp.float32)],
        [],
        [in_any] + [in_vmem] * 2,
        [in_vmem],
        "output_gate",
    )(away, normed, gate_out)
    partners = [swapped_left(opened, second[0], second[3]), swapped_left(opened, second[1], second[2])]
    parts = [second[0], second[3], second[1], second[2]]
    last = call(
        last_contract_kernel,
        [array((late, tile_rows, tile_cols))] * 8,
        [vmem((late, 2, depth, tile_cols), small)],
        [in_vmem] * 6,
        [in_vmem] * 8,
        "contract",
    )(*partners, *parts)
    aways = [exchanged(last[mask], 4 ^ mask) for mask in (0, 3, 2, 1)]
    totals = call(
        add_kernel,
        [array((early + late, tile_rows, tile_cols))] * 4,
        [vmem(shape, small)],
        [in_vmem] * 6,
        [in_vmem] * 4,
        "add_halves",
    )(keep, arrived, *last[4:])
    totals = spread(totals)
    (update,) = call(
        functools.partial(finish_kernel, 8, chunk_sizes),
        [array(pair.shape)],
        [vmem(pair.shape, small), semaphores((tile_rows // 8,))],
        [in_vmem] * 12,
        [in_any],
        "norm_and_project_out",
    )(*aways, *totals, opened, norm_out_gain[None], norm_out_bias[None], proj_out)
    return update


def solution(mesh):
    placed = (P(("grp", "row"), "col", None), P("grp"), P(), P(), P(), P(), P(), P(), P(), P())
    return jax.shard_map(
        shards_by_halves if mesh.shape["row"] == 8 else shards_by_exchange,
        mesh=mesh,
        in_specs=placed,
        out_specs=P(("grp", "row"), "col", None),
        check_vma=False,
    )
```

```python
import functools

import jax
import jax.numpy as jnp
from jax import lax
from jax.experimental import pallas as pl
from jax.experimental.pallas import tpu as pltpu
from jax.sharding import PartitionSpec as P

epsilon = 1e-05
chunk_sizes = (13, 19)
away_masks = (3, 2, 1, 0)
return_masks = (0, 3, 2, 1)
vmem_all = 60 * 1024 * 1024
vmem_part = 28 * 1024 * 1024


def from_partner(value, axis, apart):
    mask = 2**apart
    pairs = [(source, source ^ mask) for source in range(lax.axis_size(axis))]
    return lax.ppermute(value, axis, pairs)


def normalize_in(pair, gain, bias):
    widened = pair.astype(jnp.float32)
    average = jnp.mean(widened, axis=-1, keepdims=True)
    centered = widened - average
    spread = jnp.mean(centered * centered, axis=-1, keepdims=True)
    return (centered * lax.rsqrt(spread + epsilon) * gain + bias).astype(jnp.bfloat16)


def token_mask(tile_rows, tile_cols, length):
    row_start = lax.axis_index("row") * tile_rows
    col_start = lax.axis_index("col") * tile_cols
    valid_rows = row_start + jnp.arange(tile_rows, dtype=jnp.int32) < length[0]
    valid_cols = col_start + jnp.arange(tile_cols, dtype=jnp.int32) < length[0]
    return (valid_rows[:, None] & valid_cols[None, :]).astype(jnp.float32)


def make_edges(normed, proj, gate, mask):
    projected = jnp.einsum("ijc,ch->hij", normed, proj, preferred_element_type=jnp.float32)
    gating = jnp.einsum("ijc,ch->hij", normed, gate, preferred_element_type=jnp.float32)
    return (jax.nn.sigmoid(gating) * projected * mask[None]).astype(jnp.bfloat16)


def finish(contracted, normed, gate_out, gain, bias, proj_out):
    widened = contracted.astype(jnp.float32)
    average = jnp.mean(widened, axis=0, keepdims=True)
    centered = widened - average
    spread = jnp.mean(centered * centered, axis=0, keepdims=True)
    scaled = centered * lax.rsqrt(spread + epsilon) * gain[:, None, None]
    contracted_norm = (scaled + bias[:, None, None]).astype(jnp.bfloat16)
    out_gate = jax.nn.sigmoid(
        jnp.einsum("ijc,cd->ijd", normed, gate_out, preferred_element_type=jnp.float32)
    )
    projected_out = jnp.einsum(
        "hij,hc->ijc", contracted_norm, proj_out, preferred_element_type=jnp.float32
    )
    return (out_gate * projected_out).astype(jnp.bfloat16)


def contract(left, right):
    return jnp.einsum("hki,hkj->hij", left, right, preferred_element_type=jnp.float32)


def shards_by_exchange(
    pair,
    length,
    norm_in_gain,
    norm_in_bias,
    proj_in,
    gate_in,
    gate_out,
    norm_out_gain,
    norm_out_bias,
    proj_out,
):
    hidden = proj_out.shape[0]
    normed = normalize_in(pair, norm_in_gain, norm_in_bias)
    mask = token_mask(pair.shape[0], pair.shape[1], length)
    edges = make_edges(normed, proj_in, gate_in, mask)
    left_rows = lax.all_to_all(edges[:hidden], "row", split_axis=0, concat_axis=1, tiled=True)
    right_rows = lax.all_to_all(edges[hidden:], "row", split_axis=0, concat_axis=1, tiled=True)
    other_half = from_partner(left_rows, "col", 0)
    first_col = lax.axis_index("col") == 0
    left_full = jnp.where(
        first_col,
        jnp.concatenate([left_rows, other_half], axis=2),
        jnp.concatenate([other_half, left_rows], axis=2),
    )
    contracted = contract(left_full, right_rows).astype(jnp.bfloat16)
    returned = lax.all_to_all(contracted, "row", split_axis=1, concat_axis=0, tiled=True)
    return finish(returned, normed, gate_out, norm_out_gain, norm_out_bias, proj_out)


in_smem = pl.BlockSpec(memory_space=pltpu.SMEM)
in_any = pl.BlockSpec(memory_space=pl.ANY)
in_vmem = pl.BlockSpec(memory_space=pltpu.VMEM)
matmul_tn = (((0,), (0,)), ((), ()))
matmul_nt = (((1,), (1,)), ((), ()))


def call(kernel, outputs, scratch, specs, out_specs, name, limit=vmem_part):
    return pl.pallas_call(
        kernel,
        out_shape=outputs,
        in_specs=specs,
        out_specs=out_specs,
        scratch_shapes=scratch,
        compiler_params=pltpu.CompilerParams(vmem_limit_bytes=limit),
        name=name,
    )


def array(shape, dtype=jnp.bfloat16):
    return jax.ShapeDtypeStruct(shape, dtype)


def load(source, target, sem):
    copy = pltpu.make_async_copy(source, target, sem)
    copy.start()
    return copy


def chosen_weights(start, size, slots, row, proj, gate):
    width = proj.shape[1]
    first_slot, slot_count = slots
    count = 2 * slot_count * size
    at = lax.broadcasted_iota(jnp.int32, (count, width), 0)
    side, inside = at // (slot_count * size), at % (slot_count * size)
    slot, channel = first_slot + inside // size, inside % size
    source = side * (width // 2) + start + ((row % 4) ^ slot) * size + channel
    one_hot = (lax.broadcasted_iota(jnp.int32, (count, width), 1) == source).astype(jnp.bfloat16)
    picked = [
        lax.dot_general(one_hot, weights, matmul_nt, preferred_element_type=jnp.float32)
        for weights in (proj, gate)
    ]
    return jnp.concatenate(picked, axis=0).astype(jnp.bfloat16)


def block_edges(length, normed, weights, at, row_start, col_start, outs):
    rows, tile_cols, channels = normed.shape
    size = outs[0].shape[0] // 2
    pairs = lax.dot_general(
        weights,
        normed.reshape(rows * tile_cols, channels),
        matmul_nt,
        preferred_element_type=jnp.float32,
    )
    count = pairs.shape[0] // 2
    values = jax.nn.sigmoid(pairs[count:]) * pairs[:count]
    cols = col_start + lax.broadcasted_iota(jnp.int32, (count, tile_cols), 1)
    masked = []
    for row in range(rows):
        limit = jnp.where(row_start + at + row < length, length, 0)
        piece = values[:, row * tile_cols : (row + 1) * tile_cols]
        masked.append(jnp.where(cols < limit, piece, 0.0))
    swapped = jnp.swapaxes(jnp.stack(masked, axis=0), 0, 1).astype(jnp.bfloat16)
    for slot, out in enumerate(outs):
        for side in range(2):
            first = (side * len(outs) + slot) * size
            out[side * size : (side + 1) * size, at : at + rows, :] = swapped[first : first + size]


def first_kernel(bounds, length, pair, gain, bias, proj, gate, normed, *rest):
    start, size, rows = bounds
    outs = rest[:3]
    pair_held, gain_held, bias_held, proj_held, gate_held, normed_held = rest[3:9]
    helds, sems = rest[9:12], rest[12]
    tile_rows, tile_cols, channels = pair.shape
    blocks = tile_rows // rows
    parts = [pl.ds(b * rows, rows) for b in range(blocks)]
    pieces = [load(pair.at[p], pair_held.at[p], sems.at[b, 0]) for b, p in enumerate(parts)]
    small = [
        load(source, target, sems.at[blocks, at])
        for at, (source, target) in enumerate(
            ((proj, proj_held), (gate, gate_held), (gain, gain_held), (bias, bias_held))
        )
    ]
    row = lax.axis_index("row")
    row_start = row * tile_rows
    col_start = lax.axis_index("col") * tile_cols
    for copy in small:
        copy.wait()
    weights = chosen_weights(start, size, (1, 3), row, proj_held[...], gate_held[...])
    mean = jnp.full((channels, channels), 1.0 / channels, jnp.bfloat16)
    stores = []
    for b, part in enumerate(parts):
        at = b * rows
        pieces[b].wait()
        tokens = pair_held[at : at + rows].reshape(rows * tile_cols, channels)
        average = jnp.dot(tokens, mean, preferred_element_type=jnp.float32)
        centered = tokens.astype(jnp.float32) - average
        spread = jnp.mean(centered * centered, axis=-1, keepdims=True)
        scaled = centered * lax.rsqrt(spread + epsilon) * gain_held[...] + bias_held[...]
        rounded = scaled.astype(jnp.bfloat16).reshape(rows, tile_cols, channels)
        normed_held[at : at + rows] = rounded
        stores.append(load(normed_held.at[part], normed.at[part], sems.at[b, 1]))
        block_edges(length[0], rounded, weights, at, row_start, col_start, helds)
        for slot, out in enumerate(outs):
            stores.append(load(helds[slot].at[:, part], out.at[:, part], sems.at[b, 2 + slot]))
    for copy in stores:
        copy.wait()


def later_kernel(bounds, length, normed, proj, gate, *outs):
    rows, *chunks = bounds
    tile_rows, tile_cols, _ = normed.shape
    row = lax.axis_index("row")
    row_start = row * tile_rows
    col_start = lax.axis_index("col") * tile_cols
    for start, size, slots in chunks:
        weights = chosen_weights(start, size, slots, row, proj[...], gate[...])
        for at in range(0, tile_rows, rows):
            tokens = normed[at : at + rows]
            targets = outs[: slots[1]]
            block_edges(length[0], tokens, weights, at, row_start, col_start, targets)
        outs = outs[slots[1] :]


def gate_kernel(rows, after, normed, weights, out):
    tile_rows, tile_cols, channels = normed.shape
    for at in range(0, tile_rows, rows):
        gating = jnp.dot(
            normed[at : at + rows].reshape(rows * tile_cols, channels),
            weights[...],
            preferred_element_type=jnp.float32,
        )
        out[at : at + rows] = jax.nn.sigmoid(gating).reshape(rows, tile_cols, channels)


def pack_kernel(after, a, b, out, sems):
    size, count, _ = out.shape
    part = count // 2
    copies = [
        load(ref.at[pl.ds(0, size)], out.at[:, pl.ds(at * part, part), :], sems.at[at])
        for at, ref in enumerate((a, b))
    ]
    for copy in copies:
        copy.wait()


def contractions(partners, parts, store):
    size = parts[0].shape[0] // 2
    low = lax.axis_index("row") < 4
    own_away = (lax.axis_index("col") == 1) == low

    def both(first):
        for u in range(size):
            right = jnp.concatenate([part[size + u] for part in parts], axis=0)
            own = jnp.concatenate([part[u] for part in parts], axis=0)
            theirs = jnp.concatenate([partner[u] for partner in partners], axis=0)
            for side in range(2):
                left = theirs if first ^ side else own
                product = lax.dot_general(
                    left, right, matmul_tn, preferred_element_type=jnp.float32
                )
                store(u, side, product)

    pl.when(own_away)(functools.partial(both, 0))
    pl.when(jnp.logical_not(own_away))(functools.partial(both, 1))


def contract_kernel(*refs):
    partners, parts, outs = refs[:2], refs[2:6], refs[6:]

    def store(u, side, product):
        outs[side][u] = product.astype(outs[side].dtype)

    contractions(partners, parts, store)


def last_contract_kernel(*refs):
    partners, parts = refs[:2], refs[2:6]
    outs, held = (refs[6:10], refs[10:14]), refs[14]
    part = outs[0][0].shape[1]
    row = lax.axis_index("row")

    def store(u, side, product):
        held[u, side] = product.astype(jnp.bfloat16)
        for slot, out in enumerate(outs[side]):
            rows = pl.ds(pl.multiple_of(((row % 4) ^ slot) * part, part), part)
            out[u] = held[u, side, rows, :]

    contractions(partners, parts, store)


def add_kernel(keep, arrived, *refs):
    lasts, outs, held = refs[:4], refs[4:8], refs[8]
    size, part = keep.shape[0], outs[0].shape[1]
    row = lax.axis_index("row")
    held[...] = (keep[...] + arrived[...].astype(jnp.float32)).astype(jnp.bfloat16)
    for slot, (last, out) in enumerate(zip(lasts, outs, strict=True)):
        rows = pl.ds(pl.multiple_of(((row % 4) ^ slot) * part, part), part)
        out[:size] = held[:, rows, :]
        out[size:] = last[...]


def finish_kernel(rows, sizes, *refs):
    aways = [refs[away_masks.index(apart)] for apart in return_masks]
    totals = refs[4:8]
    opened, gain, bias, proj, out, out_held, sems = refs[8:]
    early, late = sizes
    tile_rows = out.shape[0]
    hidden, per = proj.shape[0], early + late
    row = lax.axis_index("row")
    at = lax.broadcasted_iota(jnp.int32, (hidden, hidden), 0)
    slot, place = at // per, at % per
    mask = sum(jnp.where(slot == place, apart, 0) for place, apart in enumerate(return_masks))
    owner = (row % 4) ^ mask
    channel = jnp.where(
        place < early, owner * early + place, 4 * early + owner * late + place - early
    )
    picked = lax.broadcasted_iota(jnp.int32, (hidden, hidden), 1) == channel

    def down(values):
        column = jnp.sum(jnp.where(picked, values, 0.0), axis=1, keepdims=True)
        return jnp.broadcast_to(column, (hidden, hidden))[None]

    gain_rows, bias_rows = down(gain[...]), down(bias[...])
    ordered = jnp.dot(
        picked.astype(jnp.bfloat16), proj[...], preferred_element_type=jnp.float32
    ).astype(jnp.bfloat16)
    stores = []
    for b in range(tile_rows // rows):
        own = slice(b * rows, (b + 1) * rows)
        pieces = []
        for total, away in zip(totals, aways, strict=True):
            pieces.append(total[:early, own, :].astype(jnp.float32))
            kept = total[early:, own, :].astype(jnp.float32)
            pieces.append(kept + away[:, own, :].astype(jnp.float32))
        values = jnp.concatenate(pieces, axis=0)
        centered = values - jnp.sum(values, axis=0, keepdims=True) * (1.0 / hidden)
        spread = jnp.sum(centered * centered, axis=0, keepdims=True) * (1.0 / hidden)
        swapped = jnp.swapaxes(centered * lax.rsqrt(spread + epsilon), 0, 1)
        scaled = (swapped * gain_rows + bias_rows).astype(jnp.bfloat16)
        for step in range(rows):
            projected = lax.dot_general(
                scaled[step], ordered, matmul_tn, preferred_element_type=jnp.float32
            )
            at_row = b * rows + step
            out_held[at_row] = (opened[at_row] * projected).astype(jnp.bfloat16)
        part = pl.ds(b * rows, rows)
        stores.append(load(out_held.at[part], out.at[part], sems.at[b]))
    for copy in stores:
        copy.wait()


def shards_by_halves(
    pair,
    length,
    norm_in_gain,
    norm_in_bias,
    proj_in,
    gate_in,
    gate_out,
    norm_out_gain,
    norm_out_bias,
    proj_out,
):
    tile_rows, tile_cols, channels = pair.shape
    rows = lax.axis_size("row")
    block = min(16, tile_rows)
    blocks = tile_rows // block
    early, late = chunk_sizes
    vmem, semaphores = pltpu.VMEM, pltpu.SemaphoreType.DMA
    small = jnp.bfloat16
    depth = 4 * tile_rows

    def exchanged(value, mask):
        return lax.ppermute(value, "row", [(source, source ^ mask) for source in range(rows)])

    def edge_shape(size):
        return (2 * size, tile_rows, tile_cols)

    def spread(pieces):
        return [pieces[0], *[exchanged(pieces[mask], mask) for mask in (3, 2, 1)]]

    def swapped_left(after, a, b):
        (left,) = call(
            pack_kernel,
            [array((a.shape[0] // 2, depth // 2, tile_cols))],
            [semaphores((2,))],
            [in_any] * 3,
            [in_any],
            "pack_left",
        )(after, a, b)
        return from_partner(left, "col", 0)

    normed, *sent = call(
        functools.partial(first_kernel, (0, early, block)),
        [array(pair.shape), *[array(edge_shape(early))] * 3],
        [
            vmem(pair.shape, small),
            vmem((1, channels), jnp.float32),
            vmem((1, channels), jnp.float32),
            vmem(proj_in.shape, small),
            vmem(gate_in.shape, small),
            vmem(pair.shape, small),
            *[vmem(edge_shape(early), small)] * 3,
            semaphores((blocks + 1, 5)),
        ],
        [in_smem] + [in_any] * 5,
        [in_any] * 4,
        "norm_and_first_edges",
        vmem_all,
    )(length, pair, norm_in_gain[None], norm_in_bias[None], proj_in, gate_in)
    own, *second = call(
        functools.partial(later_kernel, (block, (0, early, (0, 1)), (4 * early, late, (0, 4)))),
        [array(edge_shape(early)), *[array(edge_shape(late))] * 4],
        [],
        [in_smem] + [in_vmem] * 3,
        [in_vmem] * 5,
        "later_edges",
    )(length, normed, proj_in, gate_in)
    first = spread([own, *sent])
    partners = [swapped_left(second[0], first[0], first[3]), swapped_left(second[0], first[1], first[2])]
    parts = [first[0], first[3], first[1], first[2]]
    shape = (early, depth, tile_cols)
    away, keep = call(
        contract_kernel,
        [array(shape), array(shape, jnp.float32)],
        [],
        [in_vmem] * 6,
        [in_vmem] * 2,
        "contract",
    )(*partners, *parts)
    arrived = exchanged(away, 4)
    second = spread(second)
    (opened,) = call(
        functools.partial(gate_kernel, block),
        [array(pair.shape, jnp.float32)],
        [],
        [in_any] + [in_vmem] * 2,
        [in_vmem],
        "output_gate",
    )(away, normed, gate_out)
    partners = [swapped_left(opened, second[0], second[3]), swapped_left(opened, second[1], second[2])]
    parts = [second[0], second[3], second[1], second[2]]
    last = call(
        last_contract_kernel,
        [array((late, tile_rows, tile_cols))] * 8,
        [vmem((late, 2, depth, tile_cols), small)],
        [in_vmem] * 6,
        [in_vmem] * 8,
        "contract",
    )(*partners, *parts)
    aways = [exchanged(last[mask], 4 ^ mask) for mask in away_masks]
    totals = call(
        add_kernel,
        [array((early + late, tile_rows, tile_cols))] * 4,
        [vmem(shape, small)],
        [in_vmem] * 6,
        [in_vmem] * 4,
        "add_halves",
    )(keep, arrived, *last[4:])
    totals = [totals[0], *[exchanged(totals[mask], mask) for mask in return_masks[1:]]]
    (update,) = call(
        functools.partial(finish_kernel, 8, chunk_sizes),
        [array(pair.shape)],
        [vmem(pair.shape, small), semaphores((tile_rows // 8,))],
        [in_vmem] * 12,
        [in_any],
        "norm_and_project_out",
    )(*aways, *totals, opened, norm_out_gain[None], norm_out_bias[None], proj_out)
    return update


def solution(mesh):
    placed = (P(("grp", "row"), "col", None), P("grp"), P(), P(), P(), P(), P(), P(), P(), P())
    return jax.shard_map(
        shards_by_halves if mesh.shape["row"] == 8 else shards_by_exchange,
        mesh=mesh,
        in_specs=placed,
        out_specs=P(("grp", "row"), "col", None),
        check_vma=False,
    )
```

```python
import functools

import jax
import jax.numpy as jnp
from jax import lax
from jax.experimental import pallas as pl
from jax.experimental.pallas import tpu as pltpu
from jax.sharding import PartitionSpec as P

epsilon = 1e-05
chunk_sizes = (13, 19)
away_masks = (3, 2, 1, 0)
return_masks = (0, 3, 2, 1)
vmem_all = 60 * 1024 * 1024
vmem_part = 28 * 1024 * 1024


def from_partner(value, axis, apart):
    mask = 2**apart
    pairs = [(source, source ^ mask) for source in range(lax.axis_size(axis))]
    return lax.ppermute(value, axis, pairs)


def normalize_in(pair, gain, bias):
    widened = pair.astype(jnp.float32)
    average = jnp.mean(widened, axis=-1, keepdims=True)
    centered = widened - average
    spread = jnp.mean(centered * centered, axis=-1, keepdims=True)
    return (centered * lax.rsqrt(spread + epsilon) * gain + bias).astype(jnp.bfloat16)


def token_mask(tile_rows, tile_cols, length):
    row_start = lax.axis_index("row") * tile_rows
    col_start = lax.axis_index("col") * tile_cols
    valid_rows = row_start + jnp.arange(tile_rows, dtype=jnp.int32) < length[0]
    valid_cols = col_start + jnp.arange(tile_cols, dtype=jnp.int32) < length[0]
    return (valid_rows[:, None] & valid_cols[None, :]).astype(jnp.float32)


def make_edges(normed, proj, gate, mask):
    projected = jnp.einsum("ijc,ch->hij", normed, proj, preferred_element_type=jnp.float32)
    gating = jnp.einsum("ijc,ch->hij", normed, gate, preferred_element_type=jnp.float32)
    return (jax.nn.sigmoid(gating) * projected * mask[None]).astype(jnp.bfloat16)


def finish(contracted, normed, gate_out, gain, bias, proj_out):
    widened = contracted.astype(jnp.float32)
    average = jnp.mean(widened, axis=0, keepdims=True)
    centered = widened - average
    spread = jnp.mean(centered * centered, axis=0, keepdims=True)
    scaled = centered * lax.rsqrt(spread + epsilon) * gain[:, None, None]
    contracted_norm = (scaled + bias[:, None, None]).astype(jnp.bfloat16)
    out_gate = jax.nn.sigmoid(
        jnp.einsum("ijc,cd->ijd", normed, gate_out, preferred_element_type=jnp.float32)
    )
    projected_out = jnp.einsum(
        "hij,hc->ijc", contracted_norm, proj_out, preferred_element_type=jnp.float32
    )
    return (out_gate * projected_out).astype(jnp.bfloat16)


def contract(left, right):
    return jnp.einsum("hki,hkj->hij", left, right, preferred_element_type=jnp.float32)


def shards_by_exchange(
    pair,
    length,
    norm_in_gain,
    norm_in_bias,
    proj_in,
    gate_in,
    gate_out,
    norm_out_gain,
    norm_out_bias,
    proj_out,
):
    hidden = proj_out.shape[0]
    normed = normalize_in(pair, norm_in_gain, norm_in_bias)
    mask = token_mask(pair.shape[0], pair.shape[1], length)
    edges = make_edges(normed, proj_in, gate_in, mask)
    left_rows = lax.all_to_all(edges[:hidden], "row", split_axis=0, concat_axis=1, tiled=True)
    right_rows = lax.all_to_all(edges[hidden:], "row", split_axis=0, concat_axis=1, tiled=True)
    other_half = from_partner(left_rows, "col", 0)
    first_col = lax.axis_index("col") == 0
    left_full = jnp.where(
        first_col,
        jnp.concatenate([left_rows, other_half], axis=2),
        jnp.concatenate([other_half, left_rows], axis=2),
    )
    contracted = contract(left_full, right_rows).astype(jnp.bfloat16)
    returned = lax.all_to_all(contracted, "row", split_axis=1, concat_axis=0, tiled=True)
    return finish(returned, normed, gate_out, norm_out_gain, norm_out_bias, proj_out)


in_smem = pl.BlockSpec(memory_space=pltpu.SMEM)
in_any = pl.BlockSpec(memory_space=pl.ANY)
in_vmem = pl.BlockSpec(memory_space=pltpu.VMEM)
matmul_tn = (((0,), (0,)), ((), ()))
matmul_nt = (((1,), (1,)), ((), ()))


def call(kernel, outputs, scratch, specs, out_specs, name, limit=vmem_part):
    return pl.pallas_call(
        kernel,
        out_shape=outputs,
        in_specs=specs,
        out_specs=out_specs,
        scratch_shapes=scratch,
        compiler_params=pltpu.CompilerParams(vmem_limit_bytes=limit),
        name=name,
    )


def array(shape, dtype=jnp.bfloat16):
    return jax.ShapeDtypeStruct(shape, dtype)


def load(source, target, sem):
    copy = pltpu.make_async_copy(source, target, sem)
    copy.start()
    return copy


def chosen_weights(start, size, slots, row, proj, gate):
    width = proj.shape[1]
    first_slot, slot_count = slots
    count = 2 * slot_count * size
    at = lax.broadcasted_iota(jnp.int32, (count, width), 0)
    side, inside = at // (slot_count * size), at % (slot_count * size)
    slot, channel = first_slot + inside // size, inside % size
    source = side * (width // 2) + start + ((row % 4) ^ slot) * size + channel
    one_hot = (lax.broadcasted_iota(jnp.int32, (count, width), 1) == source).astype(jnp.bfloat16)
    picked = [
        lax.dot_general(one_hot, weights, matmul_nt, preferred_element_type=jnp.float32)
        for weights in (proj, gate)
    ]
    return jnp.concatenate(picked, axis=0).astype(jnp.bfloat16)


def block_edges(length, normed, weights, at, row_start, col_start, outs):
    rows, tile_cols, channels = normed.shape
    size = outs[0].shape[0] // 2
    pairs = lax.dot_general(
        weights,
        normed.reshape(rows * tile_cols, channels),
        matmul_nt,
        preferred_element_type=jnp.float32,
    )
    count = pairs.shape[0] // 2
    values = jax.nn.sigmoid(pairs[count:]) * pairs[:count]
    cols = col_start + lax.broadcasted_iota(jnp.int32, (count, tile_cols), 1)
    masked = []
    for row in range(rows):
        limit = jnp.where(row_start + at + row < length, length, 0)
        piece = values[:, row * tile_cols : (row + 1) * tile_cols]
        masked.append(jnp.where(cols < limit, piece, 0.0))
    swapped = jnp.swapaxes(jnp.stack(masked, axis=0), 0, 1).astype(jnp.bfloat16)
    for slot, out in enumerate(outs):
        for side in range(2):
            first = (side * len(outs) + slot) * size
            out[side * size : (side + 1) * size, at : at + rows, :] = swapped[first : first + size]


def first_kernel(bounds, length, pair, gain, bias, proj, gate, normed, *rest):
    start, size, rows = bounds
    outs = rest[:3]
    pair_held, gain_held, bias_held, proj_held, gate_held, normed_held = rest[3:9]
    helds, sems = rest[9:12], rest[12]
    tile_rows, tile_cols, channels = pair.shape
    blocks = tile_rows // rows
    parts = [pl.ds(b * rows, rows) for b in range(blocks)]
    pieces = [load(pair.at[p], pair_held.at[p], sems.at[b, 0]) for b, p in enumerate(parts)]
    small = [
        load(source, target, sems.at[blocks, at])
        for at, (source, target) in enumerate(
            ((proj, proj_held), (gate, gate_held), (gain, gain_held), (bias, bias_held))
        )
    ]
    row = lax.axis_index("row")
    row_start = row * tile_rows
    col_start = lax.axis_index("col") * tile_cols
    for copy in small:
        copy.wait()
    weights = chosen_weights(start, size, (1, 3), row, proj_held[...], gate_held[...])
    mean = jnp.full((channels, channels), 1.0 / channels, jnp.bfloat16)
    stores = []
    for b, part in enumerate(parts):
        at = b * rows
        pieces[b].wait()
        tokens = pair_held[at : at + rows].reshape(rows * tile_cols, channels)
        average = jnp.dot(tokens, mean, preferred_element_type=jnp.float32)
        centered = tokens.astype(jnp.float32) - average
        spread = jnp.mean(centered * centered, axis=-1, keepdims=True)
        scaled = centered * lax.rsqrt(spread + epsilon) * gain_held[...] + bias_held[...]
        rounded = scaled.astype(jnp.bfloat16).reshape(rows, tile_cols, channels)
        normed_held[at : at + rows] = rounded
        stores.append(load(normed_held.at[part], normed.at[part], sems.at[b, 1]))
        block_edges(length[0], rounded, weights, at, row_start, col_start, helds)
        for slot, out in enumerate(outs):
            stores.append(load(helds[slot].at[:, part], out.at[:, part], sems.at[b, 2 + slot]))
    for copy in stores:
        copy.wait()


def later_kernel(bounds, length, normed, proj, gate, *outs):
    rows, *chunks = bounds
    tile_rows, tile_cols, _ = normed.shape
    row = lax.axis_index("row")
    row_start = row * tile_rows
    col_start = lax.axis_index("col") * tile_cols
    for start, size, slots in chunks:
        weights = chosen_weights(start, size, slots, row, proj[...], gate[...])
        for at in range(0, tile_rows, rows):
            tokens = normed[at : at + rows]
            targets = outs[: slots[1]]
            block_edges(length[0], tokens, weights, at, row_start, col_start, targets)
        outs = outs[slots[1] :]


def gate_kernel(rows, after, normed, weights, out):
    tile_rows, tile_cols, channels = normed.shape
    for at in range(0, tile_rows, rows):
        gating = jnp.dot(
            normed[at : at + rows].reshape(rows * tile_cols, channels),
            weights[...],
            preferred_element_type=jnp.float32,
        )
        out[at : at + rows] = jax.nn.sigmoid(gating).reshape(rows, tile_cols, channels)


def pack_kernel(after, a, b, out, sems):
    size, count, _ = out.shape
    part = count // 2
    copies = [
        load(ref.at[pl.ds(0, size)], out.at[:, pl.ds(at * part, part), :], sems.at[at])
        for at, ref in enumerate((a, b))
    ]
    for copy in copies:
        copy.wait()


def contractions(partners, parts, store):
    size = parts[0].shape[0] // 2
    low = lax.axis_index("row") < 4
    own_away = (lax.axis_index("col") == 1) == low

    def both(first):
        for u in range(size):
            right = jnp.concatenate([part[size + u] for part in parts], axis=0)
            own = jnp.concatenate([part[u] for part in parts], axis=0)
            theirs = jnp.concatenate([partner[u] for partner in partners], axis=0)
            for side in range(2):
                left = theirs if first ^ side else own
                product = lax.dot_general(
                    left, right, matmul_tn, preferred_element_type=jnp.float32
                )
                store(u, side, product)

    pl.when(own_away)(functools.partial(both, 0))
    pl.when(jnp.logical_not(own_away))(functools.partial(both, 1))


def contract_kernel(*refs):
    partners, parts, outs = refs[:2], refs[2:6], refs[6:]

    def store(u, side, product):
        outs[side][u] = product.astype(outs[side].dtype)

    contractions(partners, parts, store)


def last_contract_kernel(*refs):
    partners, parts = refs[:2], refs[2:6]
    outs, held = (refs[6:10], refs[10:14]), refs[14]
    part = outs[0][0].shape[1]
    row = lax.axis_index("row")

    def store(u, side, product):
        held[u, side] = product.astype(jnp.bfloat16)
        for slot, out in enumerate(outs[side]):
            rows = pl.ds(pl.multiple_of(((row % 4) ^ slot) * part, part), part)
            out[u] = held[u, side, rows, :]

    contractions(partners, parts, store)


def add_kernel(keep, arrived, *refs):
    lasts, outs, held = refs[:4], refs[4:8], refs[8]
    size, part = keep.shape[0], outs[0].shape[1]
    row = lax.axis_index("row")
    held[...] = (keep[...] + arrived[...].astype(jnp.float32)).astype(jnp.bfloat16)
    for slot, (last, out) in enumerate(zip(lasts, outs, strict=True)):
        rows = pl.ds(pl.multiple_of(((row % 4) ^ slot) * part, part), part)
        out[:size] = held[:, rows, :]
        out[size:] = last[...]


def finish_kernel(rows, sizes, *refs):
    aways = [refs[away_masks.index(apart)] for apart in return_masks]
    totals = refs[4:8]
    opened, gain, bias, proj, out, out_held, sems = refs[8:]
    early, late = sizes
    tile_rows = out.shape[0]
    hidden, per = proj.shape[0], early + late
    row = lax.axis_index("row")
    at = lax.broadcasted_iota(jnp.int32, (hidden, hidden), 0)
    slot, place = at // per, at % per
    mask = sum(jnp.where(slot == place, apart, 0) for place, apart in enumerate(return_masks))
    owner = (row % 4) ^ mask
    channel = jnp.where(
        place < early, owner * early + place, 4 * early + owner * late + place - early
    )
    picked = lax.broadcasted_iota(jnp.int32, (hidden, hidden), 1) == channel

    def down(values):
        column = jnp.sum(jnp.where(picked, values, 0.0), axis=1, keepdims=True)
        return jnp.broadcast_to(column, (hidden, hidden))[None]

    gain_rows, bias_rows = down(gain[...]), down(bias[...])
    ordered = jnp.dot(
        picked.astype(jnp.bfloat16), proj[...], preferred_element_type=jnp.float32
    ).astype(jnp.bfloat16)
    stores = []
    for b in range(tile_rows // rows):
        own = slice(b * rows, (b + 1) * rows)
        pieces = []
        for total, away in zip(totals, aways, strict=True):
            pieces.append(total[:early, own, :].astype(jnp.float32))
            kept = total[early:, own, :].astype(jnp.float32)
            pieces.append(kept + away[:, own, :].astype(jnp.float32))
        values = jnp.concatenate(pieces, axis=0)
        centered = values - jnp.sum(values, axis=0, keepdims=True) * (1.0 / hidden)
        spread = jnp.sum(centered * centered, axis=0, keepdims=True) * (1.0 / hidden)
        swapped = jnp.swapaxes(centered * lax.rsqrt(spread + epsilon), 0, 1)
        scaled = (swapped * gain_rows + bias_rows).astype(jnp.bfloat16)
        for step in range(rows):
            projected = lax.dot_general(
                scaled[step], ordered, matmul_tn, preferred_element_type=jnp.float32
            )
            at_row = b * rows + step
            out_held[at_row] = (opened[at_row] * projected).astype(jnp.bfloat16)
        part = pl.ds(b * rows, rows)
        stores.append(load(out_held.at[part], out.at[part], sems.at[b]))
    for copy in stores:
        copy.wait()


def shards_by_halves(
    pair,
    length,
    norm_in_gain,
    norm_in_bias,
    proj_in,
    gate_in,
    gate_out,
    norm_out_gain,
    norm_out_bias,
    proj_out,
):
    tile_rows, tile_cols, channels = pair.shape
    rows = lax.axis_size("row")
    block = min(16, tile_rows)
    blocks = tile_rows // block
    early, late = chunk_sizes
    vmem, semaphores = pltpu.VMEM, pltpu.SemaphoreType.DMA
    small = jnp.bfloat16
    depth = 4 * tile_rows

    def exchanged(value, mask):
        return lax.ppermute(value, "row", [(source, source ^ mask) for source in range(rows)])

    def edge_shape(size):
        return (2 * size, tile_rows, tile_cols)

    def spread(pieces):
        return [pieces[0], *[exchanged(pieces[mask], mask) for mask in (3, 2, 1)]]

    def swapped_left(after, a, b):
        (left,) = call(
            pack_kernel,
            [array((a.shape[0] // 2, depth // 2, tile_cols))],
            [semaphores((2,))],
            [in_any] * 3,
            [in_any],
            "pack_left",
        )(after, a, b)
        return from_partner(left, "col", 0)

    normed, *sent = call(
        functools.partial(first_kernel, (0, early, block)),
        [array(pair.shape), *[array(edge_shape(early))] * 3],
        [
            vmem(pair.shape, small),
            vmem((1, channels), jnp.float32),
            vmem((1, channels), jnp.float32),
            vmem(proj_in.shape, small),
            vmem(gate_in.shape, small),
            vmem(pair.shape, small),
            *[vmem(edge_shape(early), small)] * 3,
            semaphores((blocks + 1, 5)),
        ],
        [in_smem] + [in_any] * 5,
        [in_any] * 4,
        "norm_and_first_edges",
        vmem_all,
    )(length, pair, norm_in_gain[None], norm_in_bias[None], proj_in, gate_in)
    own, *second = call(
        functools.partial(later_kernel, (block, (0, early, (0, 1)), (4 * early, late, (0, 4)))),
        [array(edge_shape(early)), *[array(edge_shape(late))] * 4],
        [],
        [in_smem] + [in_vmem] * 3,
        [in_vmem] * 5,
        "later_edges",
    )(length, normed, proj_in, gate_in)
    first = spread([own, *sent])
    partners = [swapped_left(second[0], first[0], first[3]), swapped_left(second[0], first[1], first[2])]
    parts = [first[0], first[3], first[1], first[2]]
    shape = (early, depth, tile_cols)
    away, keep = call(
        contract_kernel,
        [array(shape), array(shape, jnp.float32)],
        [],
        [in_vmem] * 6,
        [in_vmem] * 2,
        "contract",
    )(*partners, *parts)
    arrived = exchanged(away, 4)
    second = spread(second)
    (opened,) = call(
        functools.partial(gate_kernel, block),
        [array(pair.shape, jnp.float32)],
        [],
        [in_any] + [in_vmem] * 2,
        [in_vmem],
        "output_gate",
    )(away, normed, gate_out)
    partners = [swapped_left(opened, second[0], second[1]), swapped_left(opened, second[2], second[3])]
    parts = [second[0], second[1], second[2], second[3]]
    last = call(
        last_contract_kernel,
        [array((late, tile_rows, tile_cols))] * 8,
        [vmem((late, 2, depth, tile_cols), small)],
        [in_vmem] * 6,
        [in_vmem] * 8,
        "contract",
    )(*partners, *parts)
    aways = [exchanged(last[mask], 4 ^ mask) for mask in away_masks]
    totals = call(
        add_kernel,
        [array((early + late, tile_rows, tile_cols))] * 4,
        [vmem(shape, small)],
        [in_vmem] * 6,
        [in_vmem] * 4,
        "add_halves",
    )(keep, arrived, *last[4:])
    totals = [totals[0], *[exchanged(totals[mask], mask) for mask in return_masks[1:]]]
    (update,) = call(
        functools.partial(finish_kernel, 8, chunk_sizes),
        [array(pair.shape)],
        [vmem(pair.shape, small), semaphores((tile_rows // 8,))],
        [in_vmem] * 12,
        [in_any],
        "norm_and_project_out",
    )(*aways, *totals, opened, norm_out_gain[None], norm_out_bias[None], proj_out)
    return update


def solution(mesh):
    placed = (P(("grp", "row"), "col", None), P("grp"), P(), P(), P(), P(), P(), P(), P(), P())
    return jax.shard_map(
        shards_by_halves if mesh.shape["row"] == 8 else shards_by_exchange,
        mesh=mesh,
        in_specs=placed,
        out_specs=P(("grp", "row"), "col", None),
        check_vma=False,
    )
```

```python
import functools

import jax
import jax.numpy as jnp
from jax import lax
from jax.experimental import pallas as pl
from jax.experimental.pallas import tpu as pltpu
from jax.sharding import PartitionSpec as P

epsilon = 1e-05
chunk_sizes = (13, 19)
away_masks = (3, 2, 1, 0)
return_masks = (0, 3, 2, 1)
vmem_all = 60 * 1024 * 1024
vmem_part = 28 * 1024 * 1024


def from_partner(value, axis, apart):
    mask = 2**apart
    pairs = [(source, source ^ mask) for source in range(lax.axis_size(axis))]
    return lax.ppermute(value, axis, pairs)


def normalize_in(pair, gain, bias):
    widened = pair.astype(jnp.float32)
    average = jnp.mean(widened, axis=-1, keepdims=True)
    centered = widened - average
    spread = jnp.mean(centered * centered, axis=-1, keepdims=True)
    return (centered * lax.rsqrt(spread + epsilon) * gain + bias).astype(jnp.bfloat16)


def token_mask(tile_rows, tile_cols, length):
    row_start = lax.axis_index("row") * tile_rows
    col_start = lax.axis_index("col") * tile_cols
    valid_rows = row_start + jnp.arange(tile_rows, dtype=jnp.int32) < length[0]
    valid_cols = col_start + jnp.arange(tile_cols, dtype=jnp.int32) < length[0]
    return (valid_rows[:, None] & valid_cols[None, :]).astype(jnp.float32)


def make_edges(normed, proj, gate, mask):
    projected = jnp.einsum("ijc,ch->hij", normed, proj, preferred_element_type=jnp.float32)
    gating = jnp.einsum("ijc,ch->hij", normed, gate, preferred_element_type=jnp.float32)
    return (jax.nn.sigmoid(gating) * projected * mask[None]).astype(jnp.bfloat16)


def finish(contracted, normed, gate_out, gain, bias, proj_out):
    widened = contracted.astype(jnp.float32)
    average = jnp.mean(widened, axis=0, keepdims=True)
    centered = widened - average
    spread = jnp.mean(centered * centered, axis=0, keepdims=True)
    scaled = centered * lax.rsqrt(spread + epsilon) * gain[:, None, None]
    contracted_norm = (scaled + bias[:, None, None]).astype(jnp.bfloat16)
    out_gate = jax.nn.sigmoid(
        jnp.einsum("ijc,cd->ijd", normed, gate_out, preferred_element_type=jnp.float32)
    )
    projected_out = jnp.einsum(
        "hij,hc->ijc", contracted_norm, proj_out, preferred_element_type=jnp.float32
    )
    return (out_gate * projected_out).astype(jnp.bfloat16)


def contract(left, right):
    return jnp.einsum("hki,hkj->hij", left, right, preferred_element_type=jnp.float32)


def shards_by_exchange(
    pair,
    length,
    norm_in_gain,
    norm_in_bias,
    proj_in,
    gate_in,
    gate_out,
    norm_out_gain,
    norm_out_bias,
    proj_out,
):
    hidden = proj_out.shape[0]
    normed = normalize_in(pair, norm_in_gain, norm_in_bias)
    mask = token_mask(pair.shape[0], pair.shape[1], length)
    edges = make_edges(normed, proj_in, gate_in, mask)
    left_rows = lax.all_to_all(edges[:hidden], "row", split_axis=0, concat_axis=1, tiled=True)
    right_rows = lax.all_to_all(edges[hidden:], "row", split_axis=0, concat_axis=1, tiled=True)
    other_half = from_partner(left_rows, "col", 0)
    first_col = lax.axis_index("col") == 0
    left_full = jnp.where(
        first_col,
        jnp.concatenate([left_rows, other_half], axis=2),
        jnp.concatenate([other_half, left_rows], axis=2),
    )
    contracted = contract(left_full, right_rows).astype(jnp.bfloat16)
    returned = lax.all_to_all(contracted, "row", split_axis=1, concat_axis=0, tiled=True)
    return finish(returned, normed, gate_out, norm_out_gain, norm_out_bias, proj_out)


in_smem = pl.BlockSpec(memory_space=pltpu.SMEM)
in_any = pl.BlockSpec(memory_space=pl.ANY)
in_vmem = pl.BlockSpec(memory_space=pltpu.VMEM)
matmul_tn = (((0,), (0,)), ((), ()))
matmul_nt = (((1,), (1,)), ((), ()))


def call(kernel, outputs, scratch, specs, out_specs, name, limit=vmem_part):
    return pl.pallas_call(
        kernel,
        out_shape=outputs,
        in_specs=specs,
        out_specs=out_specs,
        scratch_shapes=scratch,
        compiler_params=pltpu.CompilerParams(vmem_limit_bytes=limit),
        name=name,
    )


def array(shape, dtype=jnp.bfloat16):
    return jax.ShapeDtypeStruct(shape, dtype)


def load(source, target, sem):
    copy = pltpu.make_async_copy(source, target, sem)
    copy.start()
    return copy


def chosen_weights(start, size, slots, row, proj, gate):
    width = proj.shape[1]
    first_slot, slot_count = slots
    count = 2 * slot_count * size
    at = lax.broadcasted_iota(jnp.int32, (count, width), 0)
    side, inside = at // (slot_count * size), at % (slot_count * size)
    slot, channel = first_slot + inside // size, inside % size
    source = side * (width // 2) + start + ((row % 4) ^ slot) * size + channel
    one_hot = (lax.broadcasted_iota(jnp.int32, (count, width), 1) == source).astype(jnp.bfloat16)
    picked = [
        lax.dot_general(one_hot, weights, matmul_nt, preferred_element_type=jnp.float32)
        for weights in (proj, gate)
    ]
    return jnp.concatenate(picked, axis=0).astype(jnp.bfloat16)


def block_edges(length, normed, weights, at, row_start, col_start, outs):
    rows, tile_cols, channels = normed.shape
    size = outs[0].shape[0] // 2
    pairs = lax.dot_general(
        weights,
        normed.reshape(rows * tile_cols, channels),
        matmul_nt,
        preferred_element_type=jnp.float32,
    )
    count = pairs.shape[0] // 2
    values = jax.nn.sigmoid(pairs[count:]) * pairs[:count]
    cols = col_start + lax.broadcasted_iota(jnp.int32, (count, tile_cols), 1)
    masked = []
    for row in range(rows):
        limit = jnp.where(row_start + at + row < length, length, 0)
        piece = values[:, row * tile_cols : (row + 1) * tile_cols]
        masked.append(jnp.where(cols < limit, piece, 0.0))
    swapped = jnp.swapaxes(jnp.stack(masked, axis=0), 0, 1).astype(jnp.bfloat16)
    for slot, out in enumerate(outs):
        for side in range(2):
            first = (side * len(outs) + slot) * size
            out[side * size : (side + 1) * size, at : at + rows, :] = swapped[first : first + size]


def first_kernel(bounds, length, pair, gain, bias, proj, gate, normed, *rest):
    start, size, rows = bounds
    outs = rest[:3]
    pair_held, gain_held, bias_held, proj_held, gate_held, normed_held = rest[3:9]
    helds, sems = rest[9:12], rest[12]
    tile_rows, tile_cols, channels = pair.shape
    blocks = tile_rows // rows
    parts = [pl.ds(b * rows, rows) for b in range(blocks)]
    pieces = [load(pair.at[p], pair_held.at[p], sems.at[b, 0]) for b, p in enumerate(parts)]
    small = [
        load(source, target, sems.at[blocks, at])
        for at, (source, target) in enumerate(
            ((proj, proj_held), (gate, gate_held), (gain, gain_held), (bias, bias_held))
        )
    ]
    row = lax.axis_index("row")
    row_start = row * tile_rows
    col_start = lax.axis_index("col") * tile_cols
    for copy in small:
        copy.wait()
    weights = chosen_weights(start, size, (1, 3), row, proj_held[...], gate_held[...])
    mean = jnp.full((channels, channels), 1.0 / channels, jnp.bfloat16)
    stores = []
    for b, part in enumerate(parts):
        at = b * rows
        pieces[b].wait()
        tokens = pair_held[at : at + rows].reshape(rows * tile_cols, channels)
        average = jnp.dot(tokens, mean, preferred_element_type=jnp.float32)
        centered = tokens.astype(jnp.float32) - average
        spread = jnp.mean(centered * centered, axis=-1, keepdims=True)
        scaled = centered * lax.rsqrt(spread + epsilon) * gain_held[...] + bias_held[...]
        rounded = scaled.astype(jnp.bfloat16).reshape(rows, tile_cols, channels)
        normed_held[at : at + rows] = rounded
        stores.append(load(normed_held.at[part], normed.at[part], sems.at[b, 1]))
        block_edges(length[0], rounded, weights, at, row_start, col_start, helds)
        for slot, out in enumerate(outs):
            stores.append(load(helds[slot].at[:, part], out.at[:, part], sems.at[b, 2 + slot]))
    for copy in stores:
        copy.wait()


def later_kernel(bounds, length, normed, proj, gate, *outs):
    rows, *chunks = bounds
    tile_rows, tile_cols, _ = normed.shape
    row = lax.axis_index("row")
    row_start = row * tile_rows
    col_start = lax.axis_index("col") * tile_cols
    for start, size, slots in chunks:
        weights = chosen_weights(start, size, slots, row, proj[...], gate[...])
        for at in range(0, tile_rows, rows):
            tokens = normed[at : at + rows]
            targets = outs[: slots[1]]
            block_edges(length[0], tokens, weights, at, row_start, col_start, targets)
        outs = outs[slots[1] :]


def gate_kernel(rows, after, normed, weights, out):
    tile_rows, tile_cols, channels = normed.shape
    for at in range(0, tile_rows, rows):
        gating = jnp.dot(
            normed[at : at + rows].reshape(rows * tile_cols, channels),
            weights[...],
            preferred_element_type=jnp.float32,
        )
        out[at : at + rows] = jax.nn.sigmoid(gating).reshape(rows, tile_cols, channels)


def pack_kernel(after, a, b, out, sems):
    size, count, _ = out.shape
    part = count // 2
    copies = [
        load(ref.at[pl.ds(0, size)], out.at[:, pl.ds(at * part, part), :], sems.at[at])
        for at, ref in enumerate((a, b))
    ]
    for copy in copies:
        copy.wait()


def contractions(partners, parts, store):
    size = parts[0].shape[0] // 2
    low = lax.axis_index("row") < 4
    own_away = (lax.axis_index("col") == 1) == low

    def both(first):
        for u in range(size):
            right = jnp.concatenate([part[size + u] for part in parts], axis=0)
            own = jnp.concatenate([part[u] for part in parts], axis=0)
            theirs = jnp.concatenate([partner[u] for partner in partners], axis=0)
            for side in range(2):
                left = theirs if first ^ side else own
                product = lax.dot_general(
                    left, right, matmul_tn, preferred_element_type=jnp.float32
                )
                store(u, side, product)

    pl.when(own_away)(functools.partial(both, 0))
    pl.when(jnp.logical_not(own_away))(functools.partial(both, 1))


def contract_kernel(*refs):
    partners, parts, outs = refs[:2], refs[2:6], refs[6:]

    def store(u, side, product):
        outs[side][u] = product.astype(outs[side].dtype)

    contractions(partners, parts, store)


def last_contract_kernel(*refs):
    partners, parts = refs[:2], refs[2:6]
    outs, held = (refs[6:10], refs[10:14]), refs[14]
    part = outs[0][0].shape[1]
    row = lax.axis_index("row")

    def store(u, side, product):
        held[u, side] = product.astype(jnp.bfloat16)
        for slot, out in enumerate(outs[side]):
            rows = pl.ds(pl.multiple_of(((row % 4) ^ slot) * part, part), part)
            out[u] = held[u, side, rows, :]

    contractions(partners, parts, store)


def add_kernel(keep, arrived, *refs):
    lasts, outs, held = refs[:4], refs[4:8], refs[8]
    size, part = keep.shape[0], outs[0].shape[1]
    row = lax.axis_index("row")
    held[...] = (keep[...] + arrived[...].astype(jnp.float32)).astype(jnp.bfloat16)
    for slot, (last, out) in enumerate(zip(lasts, outs, strict=True)):
        rows = pl.ds(pl.multiple_of(((row % 4) ^ slot) * part, part), part)
        out[:size] = held[:, rows, :]
        out[size:] = last[...]


def finish_kernel(rows, sizes, *refs):
    aways = [refs[away_masks.index(apart)] for apart in return_masks]
    totals = refs[4:8]
    opened, gain, bias, proj, out, out_held, sems = refs[8:]
    early, late = sizes
    tile_rows = out.shape[0]
    hidden, per = proj.shape[0], early + late
    row = lax.axis_index("row")
    at = lax.broadcasted_iota(jnp.int32, (hidden, hidden), 0)
    slot, place = at // per, at % per
    mask = sum(jnp.where(slot == place, apart, 0) for place, apart in enumerate(return_masks))
    owner = (row % 4) ^ mask
    channel = jnp.where(
        place < early, owner * early + place, 4 * early + owner * late + place - early
    )
    picked = lax.broadcasted_iota(jnp.int32, (hidden, hidden), 1) == channel

    def down(values):
        column = jnp.sum(jnp.where(picked, values, 0.0), axis=1, keepdims=True)
        return jnp.broadcast_to(column, (hidden, hidden))[None]

    gain_rows, bias_rows = down(gain[...]), down(bias[...])
    ordered = jnp.dot(
        picked.astype(jnp.bfloat16), proj[...], preferred_element_type=jnp.float32
    ).astype(jnp.bfloat16)
    stores = []
    for b in range(tile_rows // rows):
        own = slice(b * rows, (b + 1) * rows)
        pieces = []
        for total, away in zip(totals, aways, strict=True):
            pieces.append(total[:early, own, :].astype(jnp.float32))
            kept = total[early:, own, :].astype(jnp.float32)
            pieces.append(kept + away[:, own, :].astype(jnp.float32))
        values = jnp.concatenate(pieces, axis=0)
        centered = values - jnp.sum(values, axis=0, keepdims=True) * (1.0 / hidden)
        spread = jnp.sum(centered * centered, axis=0, keepdims=True) * (1.0 / hidden)
        swapped = jnp.swapaxes(centered * lax.rsqrt(spread + epsilon), 0, 1)
        scaled = (swapped * gain_rows + bias_rows).astype(jnp.bfloat16)
        for step in range(rows):
            projected = lax.dot_general(
                scaled[step], ordered, matmul_tn, preferred_element_type=jnp.float32
            )
            at_row = b * rows + step
            out_held[at_row] = (opened[at_row] * projected).astype(jnp.bfloat16)
        part = pl.ds(b * rows, rows)
        stores.append(load(out_held.at[part], out.at[part], sems.at[b]))
    for copy in stores:
        copy.wait()


def shards_by_halves(
    pair,
    length,
    norm_in_gain,
    norm_in_bias,
    proj_in,
    gate_in,
    gate_out,
    norm_out_gain,
    norm_out_bias,
    proj_out,
):
    tile_rows, tile_cols, channels = pair.shape
    rows = lax.axis_size("row")
    block = min(16, tile_rows)
    blocks = tile_rows // block
    early, late = chunk_sizes
    vmem, semaphores = pltpu.VMEM, pltpu.SemaphoreType.DMA
    small = jnp.bfloat16
    depth = 4 * tile_rows

    def exchanged(value, mask):
        return lax.ppermute(value, "row", [(source, source ^ mask) for source in range(rows)])

    def edge_shape(size):
        return (2 * size, tile_rows, tile_cols)

    def spread(pieces):
        return [pieces[0], *[exchanged(pieces[mask], mask) for mask in (3, 2, 1)]]

    def swapped_left(after, a, b):
        (left,) = call(
            pack_kernel,
            [array((a.shape[0] // 2, depth // 2, tile_cols))],
            [semaphores((2,))],
            [in_any] * 3,
            [in_any],
            "pack_left",
        )(after, a, b)
        return from_partner(left, "col", 0)

    normed, *sent = call(
        functools.partial(first_kernel, (0, early, block)),
        [array(pair.shape), *[array(edge_shape(early))] * 3],
        [
            vmem(pair.shape, small),
            vmem((1, channels), jnp.float32),
            vmem((1, channels), jnp.float32),
            vmem(proj_in.shape, small),
            vmem(gate_in.shape, small),
            vmem(pair.shape, small),
            *[vmem(edge_shape(early), small)] * 3,
            semaphores((blocks + 1, 5)),
        ],
        [in_smem] + [in_any] * 5,
        [in_any] * 4,
        "norm_and_first_edges",
        vmem_all,
    )(length, pair, norm_in_gain[None], norm_in_bias[None], proj_in, gate_in)
    own, *second = call(
        functools.partial(later_kernel, (block, (0, early, (0, 1)), (4 * early, late, (0, 4)))),
        [array(edge_shape(early)), *[array(edge_shape(late))] * 4],
        [],
        [in_smem] + [in_vmem] * 3,
        [in_vmem] * 5,
        "later_edges",
    )(length, normed, proj_in, gate_in)
    first = spread([own, *sent])
    partners = [swapped_left(second[0], first[0], first[3]), swapped_left(second[0], first[1], first[2])]
    parts = [first[0], first[3], first[1], first[2]]
    shape = (early, depth, tile_cols)
    away, keep = call(
        contract_kernel,
        [array(shape), array(shape, jnp.float32)],
        [],
        [in_vmem] * 6,
        [in_vmem] * 2,
        "contract",
    )(*partners, *parts)
    arrived = exchanged(away, 4)
    second = spread(second)
    (opened,) = call(
        functools.partial(gate_kernel, block),
        [array(pair.shape, jnp.float32)],
        [],
        [in_any] + [in_vmem] * 2,
        [in_vmem],
        "output_gate",
        vmem_all,
    )(away, normed, gate_out)
    partners = [swapped_left(opened, second[0], second[1]), swapped_left(opened, second[2], second[3])]
    parts = [second[0], second[1], second[2], second[3]]
    last = call(
        last_contract_kernel,
        [array((late, tile_rows, tile_cols))] * 8,
        [vmem((late, 2, depth, tile_cols), small)],
        [in_vmem] * 6,
        [in_vmem] * 8,
        "contract",
    )(*partners, *parts)
    aways = [exchanged(last[mask], 4 ^ mask) for mask in away_masks]
    totals = call(
        add_kernel,
        [array((early + late, tile_rows, tile_cols))] * 4,
        [vmem(shape, small)],
        [in_vmem] * 6,
        [in_vmem] * 4,
        "add_halves",
    )(keep, arrived, *last[4:])
    totals = [totals[0], *[exchanged(totals[mask], mask) for mask in return_masks[1:]]]
    (update,) = call(
        functools.partial(finish_kernel, 8, chunk_sizes),
        [array(pair.shape)],
        [vmem(pair.shape, small), semaphores((tile_rows // 8,))],
        [in_vmem] * 12,
        [in_any],
        "norm_and_project_out",
    )(*aways, *totals, opened, norm_out_gain[None], norm_out_bias[None], proj_out)
    return update


def solution(mesh):
    placed = (P(("grp", "row"), "col", None), P("grp"), P(), P(), P(), P(), P(), P(), P(), P())
    return jax.shard_map(
        shards_by_halves if mesh.shape["row"] == 8 else shards_by_exchange,
        mesh=mesh,
        in_specs=placed,
        out_specs=P(("grp", "row"), "col", None),
        check_vma=False,
    )
```

```python
import functools

import jax
import jax.numpy as jnp
from jax import lax
from jax.experimental import pallas as pl
from jax.experimental.pallas import tpu as pltpu
from jax.sharding import PartitionSpec as P

epsilon = 1e-05
chunk_sizes = (13, 19)
away_masks = (3, 2, 1, 0)
return_masks = (0, 3, 2, 1)
vmem_all = 60 * 1024 * 1024
vmem_part = 16 * 1024 * 1024


def from_partner(value, axis, apart):
    mask = 2**apart
    pairs = [(source, source ^ mask) for source in range(lax.axis_size(axis))]
    return lax.ppermute(value, axis, pairs)


def normalize_in(pair, gain, bias):
    widened = pair.astype(jnp.float32)
    average = jnp.mean(widened, axis=-1, keepdims=True)
    centered = widened - average
    spread = jnp.mean(centered * centered, axis=-1, keepdims=True)
    return (centered * lax.rsqrt(spread + epsilon) * gain + bias).astype(jnp.bfloat16)


def token_mask(tile_rows, tile_cols, length):
    row_start = lax.axis_index("row") * tile_rows
    col_start = lax.axis_index("col") * tile_cols
    valid_rows = row_start + jnp.arange(tile_rows, dtype=jnp.int32) < length[0]
    valid_cols = col_start + jnp.arange(tile_cols, dtype=jnp.int32) < length[0]
    return (valid_rows[:, None] & valid_cols[None, :]).astype(jnp.float32)


def make_edges(normed, proj, gate, mask):
    projected = jnp.einsum("ijc,ch->hij", normed, proj, preferred_element_type=jnp.float32)
    gating = jnp.einsum("ijc,ch->hij", normed, gate, preferred_element_type=jnp.float32)
    return (jax.nn.sigmoid(gating) * projected * mask[None]).astype(jnp.bfloat16)


def finish(contracted, normed, gate_out, gain, bias, proj_out):
    widened = contracted.astype(jnp.float32)
    average = jnp.mean(widened, axis=0, keepdims=True)
    centered = widened - average
    spread = jnp.mean(centered * centered, axis=0, keepdims=True)
    scaled = centered * lax.rsqrt(spread + epsilon) * gain[:, None, None]
    contracted_norm = (scaled + bias[:, None, None]).astype(jnp.bfloat16)
    out_gate = jax.nn.sigmoid(
        jnp.einsum("ijc,cd->ijd", normed, gate_out, preferred_element_type=jnp.float32)
    )
    projected_out = jnp.einsum(
        "hij,hc->ijc", contracted_norm, proj_out, preferred_element_type=jnp.float32
    )
    return (out_gate * projected_out).astype(jnp.bfloat16)


def contract(left, right):
    return jnp.einsum("hki,hkj->hij", left, right, preferred_element_type=jnp.float32)


def shards_by_exchange(
    pair,
    length,
    norm_in_gain,
    norm_in_bias,
    proj_in,
    gate_in,
    gate_out,
    norm_out_gain,
    norm_out_bias,
    proj_out,
):
    hidden = proj_out.shape[0]
    normed = normalize_in(pair, norm_in_gain, norm_in_bias)
    mask = token_mask(pair.shape[0], pair.shape[1], length)
    edges = make_edges(normed, proj_in, gate_in, mask)
    left_rows = lax.all_to_all(edges[:hidden], "row", split_axis=0, concat_axis=1, tiled=True)
    right_rows = lax.all_to_all(edges[hidden:], "row", split_axis=0, concat_axis=1, tiled=True)
    other_half = from_partner(left_rows, "col", 0)
    first_col = lax.axis_index("col") == 0
    left_full = jnp.where(
        first_col,
        jnp.concatenate([left_rows, other_half], axis=2),
        jnp.concatenate([other_half, left_rows], axis=2),
    )
    contracted = contract(left_full, right_rows).astype(jnp.bfloat16)
    returned = lax.all_to_all(contracted, "row", split_axis=1, concat_axis=0, tiled=True)
    return finish(returned, normed, gate_out, norm_out_gain, norm_out_bias, proj_out)


in_smem = pl.BlockSpec(memory_space=pltpu.SMEM)
in_any = pl.BlockSpec(memory_space=pl.ANY)
in_vmem = pl.BlockSpec(memory_space=pltpu.VMEM)
matmul_tn = (((0,), (0,)), ((), ()))
matmul_nt = (((1,), (1,)), ((), ()))


def call(kernel, outputs, scratch, specs, out_specs, name, limit=vmem_part):
    return pl.pallas_call(
        kernel,
        out_shape=outputs,
        in_specs=specs,
        out_specs=out_specs,
        scratch_shapes=scratch,
        compiler_params=pltpu.CompilerParams(vmem_limit_bytes=limit),
        name=name,
    )


def array(shape, dtype=jnp.bfloat16):
    return jax.ShapeDtypeStruct(shape, dtype)


def load(source, target, sem):
    copy = pltpu.make_async_copy(source, target, sem)
    copy.start()
    return copy


def chosen_weights(start, size, slots, row, proj, gate):
    width = proj.shape[1]
    first_slot, slot_count = slots
    count = 2 * slot_count * size
    at = lax.broadcasted_iota(jnp.int32, (count, width), 0)
    side, inside = at // (slot_count * size), at % (slot_count * size)
    slot, channel = first_slot + inside // size, inside % size
    source = side * (width // 2) + start + ((row % 4) ^ slot) * size + channel
    one_hot = (lax.broadcasted_iota(jnp.int32, (count, width), 1) == source).astype(jnp.bfloat16)
    picked = [
        lax.dot_general(one_hot, weights, matmul_nt, preferred_element_type=jnp.float32)
        for weights in (proj, gate)
    ]
    return jnp.concatenate(picked, axis=0).astype(jnp.bfloat16)


def block_edges(length, normed, weights, at, row_start, col_start, outs):
    rows, tile_cols, channels = normed.shape
    size = outs[0].shape[0] // 2
    pairs = lax.dot_general(
        weights,
        normed.reshape(rows * tile_cols, channels),
        matmul_nt,
        preferred_element_type=jnp.float32,
    )
    count = pairs.shape[0] // 2
    values = jax.nn.sigmoid(pairs[count:]) * pairs[:count]
    cols = col_start + lax.broadcasted_iota(jnp.int32, (count, tile_cols), 1)
    masked = []
    for row in range(rows):
        limit = jnp.where(row_start + at + row < length, length, 0)
        piece = values[:, row * tile_cols : (row + 1) * tile_cols]
        masked.append(jnp.where(cols < limit, piece, 0.0))
    swapped = jnp.swapaxes(jnp.stack(masked, axis=0), 0, 1).astype(jnp.bfloat16)
    for slot, out in enumerate(outs):
        for side in range(2):
            first = (side * len(outs) + slot) * size
            out[side * size : (side + 1) * size, at : at + rows, :] = swapped[first : first + size]


def first_kernel(bounds, length, pair, gain, bias, proj, gate, normed, *rest):
    start, size, rows = bounds
    outs = rest[:3]
    pair_held, gain_held, bias_held, proj_held, gate_held, normed_held = rest[3:9]
    helds, sems = rest[9:12], rest[12]
    tile_rows, tile_cols, channels = pair.shape
    blocks = tile_rows // rows
    parts = [pl.ds(b * rows, rows) for b in range(blocks)]
    pieces = [load(pair.at[p], pair_held.at[p], sems.at[b, 0]) for b, p in enumerate(parts)]
    small = [
        load(source, target, sems.at[blocks, at])
        for at, (source, target) in enumerate(
            ((proj, proj_held), (gate, gate_held), (gain, gain_held), (bias, bias_held))
        )
    ]
    row = lax.axis_index("row")
    row_start = row * tile_rows
    col_start = lax.axis_index("col") * tile_cols
    for copy in small:
        copy.wait()
    weights = chosen_weights(start, size, (1, 3), row, proj_held[...], gate_held[...])
    mean = jnp.full((channels, channels), 1.0 / channels, jnp.bfloat16)
    stores = []
    for b, part in enumerate(parts):
        at = b * rows
        pieces[b].wait()
        tokens = pair_held[at : at + rows].reshape(rows * tile_cols, channels)
        average = jnp.dot(tokens, mean, preferred_element_type=jnp.float32)
        centered = tokens.astype(jnp.float32) - average
        spread = jnp.mean(centered * centered, axis=-1, keepdims=True)
        scaled = centered * lax.rsqrt(spread + epsilon) * gain_held[...] + bias_held[...]
        rounded = scaled.astype(jnp.bfloat16).reshape(rows, tile_cols, channels)
        normed_held[at : at + rows] = rounded
        stores.append(load(normed_held.at[part], normed.at[part], sems.at[b, 1]))
        block_edges(length[0], rounded, weights, at, row_start, col_start, helds)
        for slot, out in enumerate(outs):
            stores.append(load(helds[slot].at[:, part], out.at[:, part], sems.at[b, 2 + slot]))
    for copy in stores:
        copy.wait()


def later_kernel(bounds, length, normed, proj, gate, *outs):
    rows, *chunks = bounds
    tile_rows, tile_cols, _ = normed.shape
    row = lax.axis_index("row")
    row_start = row * tile_rows
    col_start = lax.axis_index("col") * tile_cols
    for start, size, slots in chunks:
        weights = chosen_weights(start, size, slots, row, proj[...], gate[...])
        for at in range(0, tile_rows, rows):
            tokens = normed[at : at + rows]
            targets = outs[: slots[1]]
            block_edges(length[0], tokens, weights, at, row_start, col_start, targets)
        outs = outs[slots[1] :]


def gate_kernel(rows, after, normed, weights, out):
    tile_rows, tile_cols, channels = normed.shape
    for at in range(0, tile_rows, rows):
        gating = jnp.dot(
            normed[at : at + rows].reshape(rows * tile_cols, channels),
            weights[...],
            preferred_element_type=jnp.float32,
        )
        out[at : at + rows] = jax.nn.sigmoid(gating).reshape(rows, tile_cols, channels)


def pack_kernel(after, a, b, out, sems):
    size, count, _ = out.shape
    part = count // 2
    copies = [
        load(ref.at[pl.ds(0, size)], out.at[:, pl.ds(at * part, part), :], sems.at[at])
        for at, ref in enumerate((a, b))
    ]
    for copy in copies:
        copy.wait()


def contractions(partners, parts, store):
    size = parts[0].shape[0] // 2
    low = lax.axis_index("row") < 4
    own_away = (lax.axis_index("col") == 1) == low

    def both(first):
        for u in range(size):
            right = jnp.concatenate([part[size + u] for part in parts], axis=0)
            own = jnp.concatenate([part[u] for part in parts], axis=0)
            theirs = jnp.concatenate([partner[u] for partner in partners], axis=0)
            for side in range(2):
                left = theirs if first ^ side else own
                product = lax.dot_general(
                    left, right, matmul_tn, preferred_element_type=jnp.float32
                )
                store(u, side, product)

    pl.when(own_away)(functools.partial(both, 0))
    pl.when(jnp.logical_not(own_away))(functools.partial(both, 1))


def contract_kernel(*refs):
    partners, parts, outs = refs[:2], refs[2:6], refs[6:]

    def store(u, side, product):
        outs[side][u] = product.astype(outs[side].dtype)

    contractions(partners, parts, store)


def last_contract_kernel(*refs):
    partners, parts = refs[:2], refs[2:6]
    outs, held = (refs[6:10], refs[10:14]), refs[14]
    part = outs[0][0].shape[1]
    row = lax.axis_index("row")

    def store(u, side, product):
        held[u, side] = product.astype(jnp.bfloat16)
        for slot, out in enumerate(outs[side]):
            rows = pl.ds(pl.multiple_of(((row % 4) ^ slot) * part, part), part)
            out[u] = held[u, side, rows, :]

    contractions(partners, parts, store)


def add_kernel(keep, arrived, *refs):
    lasts, outs, held = refs[:4], refs[4:8], refs[8]
    size, part = keep.shape[0], outs[0].shape[1]
    row = lax.axis_index("row")
    held[...] = (keep[...] + arrived[...].astype(jnp.float32)).astype(jnp.bfloat16)
    for slot, (last, out) in enumerate(zip(lasts, outs, strict=True)):
        rows = pl.ds(pl.multiple_of(((row % 4) ^ slot) * part, part), part)
        out[:size] = held[:, rows, :]
        out[size:] = last[...]


def finish_kernel(rows, sizes, *refs):
    aways = [refs[away_masks.index(apart)] for apart in return_masks]
    totals = refs[4:8]
    opened, gain, bias, proj, out, out_held, sems = refs[8:]
    early, late = sizes
    tile_rows = out.shape[0]
    hidden, per = proj.shape[0], early + late
    row = lax.axis_index("row")
    at = lax.broadcasted_iota(jnp.int32, (hidden, hidden), 0)
    slot, place = at // per, at % per
    mask = sum(jnp.where(slot == place, apart, 0) for place, apart in enumerate(return_masks))
    owner = (row % 4) ^ mask
    channel = jnp.where(
        place < early, owner * early + place, 4 * early + owner * late + place - early
    )
    picked = lax.broadcasted_iota(jnp.int32, (hidden, hidden), 1) == channel

    def down(values):
        column = jnp.sum(jnp.where(picked, values, 0.0), axis=1, keepdims=True)
        return jnp.broadcast_to(column, (hidden, hidden))[None]

    gain_rows, bias_rows = down(gain[...]), down(bias[...])
    ordered = jnp.dot(
        picked.astype(jnp.bfloat16), proj[...], preferred_element_type=jnp.float32
    ).astype(jnp.bfloat16)
    stores = []
    for b in range(tile_rows // rows):
        own = slice(b * rows, (b + 1) * rows)
        pieces = []
        for total, away in zip(totals, aways, strict=True):
            pieces.append(total[:early, own, :].astype(jnp.float32))
            kept = total[early:, own, :].astype(jnp.float32)
            pieces.append(kept + away[:, own, :].astype(jnp.float32))
        values = jnp.concatenate(pieces, axis=0)
        centered = values - jnp.sum(values, axis=0, keepdims=True) * (1.0 / hidden)
        spread = jnp.sum(centered * centered, axis=0, keepdims=True) * (1.0 / hidden)
        swapped = jnp.swapaxes(centered * lax.rsqrt(spread + epsilon), 0, 1)
        scaled = (swapped * gain_rows + bias_rows).astype(jnp.bfloat16)
        for step in range(rows):
            projected = lax.dot_general(
                scaled[step], ordered, matmul_tn, preferred_element_type=jnp.float32
            )
            at_row = b * rows + step
            out_held[at_row] = (opened[at_row] * projected).astype(jnp.bfloat16)
        part = pl.ds(b * rows, rows)
        stores.append(load(out_held.at[part], out.at[part], sems.at[b]))
    for copy in stores:
        copy.wait()


def shards_by_halves(
    pair,
    length,
    norm_in_gain,
    norm_in_bias,
    proj_in,
    gate_in,
    gate_out,
    norm_out_gain,
    norm_out_bias,
    proj_out,
):
    tile_rows, tile_cols, channels = pair.shape
    rows = lax.axis_size("row")
    block = min(16, tile_rows)
    blocks = tile_rows // block
    early, late = chunk_sizes
    vmem, semaphores = pltpu.VMEM, pltpu.SemaphoreType.DMA
    small = jnp.bfloat16
    depth = 4 * tile_rows

    def exchanged(value, mask):
        return lax.ppermute(value, "row", [(source, source ^ mask) for source in range(rows)])

    def edge_shape(size):
        return (2 * size, tile_rows, tile_cols)

    def spread(pieces):
        return [pieces[0], *[exchanged(pieces[mask], mask) for mask in (3, 2, 1)]]

    def swapped_left(after, a, b):
        (left,) = call(
            pack_kernel,
            [array((a.shape[0] // 2, depth // 2, tile_cols))],
            [semaphores((2,))],
            [in_any] * 3,
            [in_any],
            "pack_left",
        )(after, a, b)
        return from_partner(left, "col", 0)

    normed, *sent = call(
        functools.partial(first_kernel, (0, early, block)),
        [array(pair.shape), *[array(edge_shape(early))] * 3],
        [
            vmem(pair.shape, small),
            vmem((1, channels), jnp.float32),
            vmem((1, channels), jnp.float32),
            vmem(proj_in.shape, small),
            vmem(gate_in.shape, small),
            vmem(pair.shape, small),
            *[vmem(edge_shape(early), small)] * 3,
            semaphores((blocks + 1, 5)),
        ],
        [in_smem] + [in_any] * 5,
        [in_any] * 4,
        "norm_and_first_edges",
        vmem_all,
    )(length, pair, norm_in_gain[None], norm_in_bias[None], proj_in, gate_in)
    own, *second = call(
        functools.partial(later_kernel, (block, (0, early, (0, 1)), (4 * early, late, (0, 4)))),
        [array(edge_shape(early)), *[array(edge_shape(late))] * 4],
        [],
        [in_smem] + [in_vmem] * 3,
        [in_vmem] * 5,
        "later_edges",
    )(length, normed, proj_in, gate_in)
    first = spread([own, *sent])
    partners = [swapped_left(second[0], first[0], first[3]), swapped_left(second[0], first[1], first[2])]
    parts = [first[0], first[3], first[1], first[2]]
    shape = (early, depth, tile_cols)
    away, keep = call(
        contract_kernel,
        [array(shape), array(shape, jnp.float32)],
        [],
        [in_vmem] * 6,
        [in_vmem] * 2,
        "contract",
    )(*partners, *parts)
    arrived = exchanged(away, 4)
    second = spread(second)
    (opened,) = call(
        functools.partial(gate_kernel, block),
        [array(pair.shape, jnp.float32)],
        [],
        [in_any] + [in_vmem] * 2,
        [in_vmem],
        "output_gate",
        vmem_all,
    )(away, normed, gate_out)
    partners = [swapped_left(opened, second[0], second[1]), swapped_left(opened, second[2], second[3])]
    parts = [second[0], second[1], second[2], second[3]]
    last = call(
        last_contract_kernel,
        [array((late, tile_rows, tile_cols))] * 8,
        [vmem((late, 2, depth, tile_cols), small)],
        [in_vmem] * 6,
        [in_vmem] * 8,
        "contract",
    )(*partners, *parts)
    aways = [exchanged(last[mask], 4 ^ mask) for mask in away_masks]
    totals = call(
        add_kernel,
        [array((early + late, tile_rows, tile_cols))] * 4,
        [vmem(shape, small)],
        [in_vmem] * 6,
        [in_vmem] * 4,
        "add_halves",
    )(keep, arrived, *last[4:])
    totals = [totals[0], *[exchanged(totals[mask], mask) for mask in return_masks[1:]]]
    (update,) = call(
        functools.partial(finish_kernel, 8, chunk_sizes),
        [array(pair.shape)],
        [vmem(pair.shape, small), semaphores((tile_rows // 8,))],
        [in_vmem] * 12,
        [in_any],
        "norm_and_project_out",
    )(*aways, *totals, opened, norm_out_gain[None], norm_out_bias[None], proj_out)
    return update


def solution(mesh):
    placed = (P(("grp", "row"), "col", None), P("grp"), P(), P(), P(), P(), P(), P(), P(), P())
    return jax.shard_map(
        shards_by_halves if mesh.shape["row"] == 8 else shards_by_exchange,
        mesh=mesh,
        in_specs=placed,
        out_specs=P(("grp", "row"), "col", None),
        check_vma=False,
    )
```
